512 devices in a mesh: scan: 64 (over y_lo, z, core), tile: 8 (over y_hi, x).
Axes of the slice: x: 4, y: 4 (y_hi: 2, y_lo: 2; y = y_hi * 2 + y_lo), z: 16, core: 2. Of those that a mesh axis runs over, the one named last changes fastest.
Arguments:
- specimen: float32 [2, 2, 1024, 512], P(None, None, 'tile'), may hold values from -6 to 6
- probe_modes: float32 [4, 2, 128, 128], P(None, None, 'tile'), may hold values from -6 to 6
- offsets: int32 [2, 512], P(None, 'scan'), may hold values from 0 to 896, as said below
- intensity: float32 [512, 128, 128], P('scan'), may hold values from 0.2 to 4
Outputs:
- specimen_grad: float32 [2, 2, 1024, 512], P(None, None, 'tile')
- probe_grad: float32 [4, 2, 128, 128], P(None, None, 'tile')
The draws below stay inside these ranges and needn't reach their ends.
Inputs may be any that keep to these rules, and one draw needn't show every extreme that they name: Let a strip be a run of 128 rows starting at a multiple of 128. Among the 8 positions of one aligned block of the batch (the positions held by one index of scan), at most 2 have their row offset in one strip, and some strip holds exactly 2 in every block. A row offset in the last strip equals 896. Column offsets lie in 0 .. 384.
All inputs are finite; a program needn't handle non-finite values.
Results may differ from the reference program's by a relative error of at most 0.0003.
Values sent between devices are 32-bit elements; how exact they have to be, the bound alone decides.
A program may use at most 64 MiB of HBM per device.

```python
import math
import jax
import jax.numpy as jnp
from jax import lax

N = 128
MODES = 4
SLICES = 2
COLS = 512
CAP = 2
BPG = 8
BATCH = 512
ROWS = 1024
N_TILE = 8


def draw_offsets(key, part):
    key = jax.random.fold_in(key, 7)
    keys = jax.random.split(key, 5)
    groups = BATCH // BPG
    others_count = max(N_TILE - 1, 1)
    busiest = jax.random.randint(keys[0], (groups, 1), 0, N_TILE)
    slot_ids = jnp.arange(BPG, dtype=jnp.int32)[None, :]
    first_other = jax.random.randint(keys[1], (groups, 1), 0, others_count)
    others = (first_other + slot_ids) % others_count
    others = others + (others >= busiest).astype(jnp.int32)
    owners = jnp.where(slot_ids < CAP, busiest, others)
    scores = jax.random.randint(keys[2], (groups, BPG), 0, 1 << 20) * BPG + slot_ids
    order = jnp.argsort(scores, axis=1)
    owners = jnp.take_along_axis(owners, order, axis=1)
    inner = jax.random.randint(keys[3], (groups, BPG), 0, N)
    inner = jnp.where(owners == N_TILE - 1, 0, inner)
    row_offsets = (owners * N + inner).reshape(-1)
    col_offsets = jax.random.randint(keys[4], (BATCH,), 0, COLS - N + 1)
    return jnp.stack([row_offsets, col_offsets]).astype(jnp.int32)


def steps_of(own_key, dims, cuts, low, top_value):
    def one(position, blocks):
        draws = jax.random.uniform(jax.random.fold_in(jax.random.fold_in(own_key, 6), position), (blocks,), jnp.float32, low / len(cuts), top_value / len(cuts))
        return jnp.repeat(jnp.exp(draws), dims[position] // blocks).reshape((-1,) + (1,) * (len(dims) - position - 1))

    level = one(*cuts[0])
    for cut in cuts[1:]:
        level = level * one(*cut)
    return level


def centred(rng, shape, width, reach, shards=(), kind=jnp.bfloat16):
    array = jax.random.normal(rng, shape, jnp.float32) * width
    if len(shards) > 0:
        array = steps_of(rng, shape, shards, -0.22, 0.18) * array
    return jnp.clip(array, min=-reach, max=reach).astype(kind)


def setup_inputs(seed: int = 0) -> dict:
    seeds = jax.random.split(jax.random.key(seed), 5)
    specimen = centred(seeds[0], (SLICES, 2, ROWS, COLS), 0.7, 6.0, ((2, 8),), jnp.float32)
    probe_modes = centred(seeds[1], (MODES, 2, N, N), 0.5, 6.0, ((2, 8),), jnp.float32)
    offsets = draw_offsets(jax.random.fold_in(seeds[4], 71), 0)
    intensity = jnp.clip(jnp.exp(math.log(4.0) - 2.9957323 * jax.random.uniform(seeds[3], (BATCH, N, N), jnp.float32) ** steps_of(seeds[3], (BATCH, N, N), ((0, 64),), -0.2, 0.2)), 0.2, 4.0)
    return {"specimen": specimen, "probe_modes": probe_modes, "offsets": offsets, "intensity": intensity}


fresnel_phase = 40.0

def position_loss(patch, probe_set, measured):
    extent = patch.shape[-1]
    frequency = jnp.fft.fftfreq(extent)
    phase_map = -fresnel_phase * (frequency[:, None] ** 2 + frequency[None, :] ** 2)
    kernel = jnp.exp(1j * phase_map)
    wavefield = probe_set[:, 0] + 1j * probe_set[:, 1]
    for depth in range(patch.shape[0]):
        wavefield = wavefield * (patch[depth, 0] + 1j * patch[depth, 1])
        if depth + 1 < patch.shape[0]:
            wavefield = jnp.fft.ifft2(kernel * jnp.fft.fft2(wavefield, norm='ortho'), norm='ortho')
    far_field = jnp.fft.fft2(wavefield, norm='ortho')
    model_int = lax.optimization_barrier(jnp.sum(jnp.real(far_field) ** 2 + jnp.imag(far_field) ** 2, axis=0))
    misfit = model_int - measured
    return 0.5 * jnp.sum(misfit * misfit)

def reference(specimen, probe_modes, offsets, intensity):
    grad_fn = jax.grad(position_loss, argnums=(0, 1))
    window = (SLICES, 2, N, N)

    def accumulate(totals, entry):
        acc_spec, acc_probe = totals
        row_at, col_at, measured = entry
        anchor = jnp.zeros((), jnp.int32)
        corner = (anchor, anchor, row_at.astype(jnp.int32), col_at.astype(jnp.int32))
        patch = lax.dynamic_slice(specimen, corner, window)
        patch_grad, probe_part = grad_fn(patch, probe_modes, measured)
        acc_spec = lax.dynamic_update_slice(acc_spec, lax.dynamic_slice(acc_spec, corner, window) + patch_grad, corner)
        return ((acc_spec, acc_probe + probe_part), None)
    initial = (jnp.zeros_like(specimen), jnp.zeros_like(probe_modes))
    finals, unused = lax.scan(accumulate, initial, (offsets[0], offsets[1], intensity))
    return (finals[0], finals[1])
```

```python
from functools import partial
import math

import jax
import jax.numpy as jnp
import numpy as np
from jax import lax
from jax.experimental import pallas as pl
from jax.experimental.pallas import tpu as pltpu
from jax.sharding import PartitionSpec as P

fresnel_phase = 40.0
F32 = jnp.float32
BF16 = jnp.bfloat16
MESH = pl.DeviceIdType.MESH
VMEM_LIMIT = 56 * 1024 * 1024
CAP = 2


def split_bf16(table):
    high = table.astype(BF16)
    low = (table - high.astype(np.float64)).astype(BF16)
    return np.asarray(high), np.asarray(low)


def dft_tables(n):
    k = np.arange(n)
    angle = (np.outer(k, k) % n) * (-2.0 * np.pi / n)
    re, im = np.cos(angle) / math.sqrt(n), np.sin(angle) / math.sqrt(n)
    forward = np.block([[re, im], [-im, re]])
    inverse = np.block([[re, -im], [im, re]])
    fh, fl = split_bf16(forward)
    ih, il = split_bf16(inverse)
    right = np.stack([np.concatenate([fh, fh, fl], 0), np.concatenate([ih, ih, il], 0)])
    left = np.stack([np.concatenate([ih, ih, il], 1), np.concatenate([fh, fh, fl], 1)])
    freq = np.fft.fftfreq(n)
    phi = -fresnel_phase * (freq[:, None] ** 2 + freq[None, :] ** 2)
    kernel = np.stack([np.cos(phi), np.sin(phi)]).astype(np.float32)
    return right, left, kernel


class Place:
    def __init__(self, ns, nt):
        self.ns, self.nt, self.nz = ns, nt, ns // 4
        s, t = lax.axis_index("scan"), lax.axis_index("tile")
        self.s, self.t = s, t
        self.core = lax.rem(s, 2)
        self.z = lax.rem(s // 2, self.nz)
        self.ylo = s // (2 * self.nz)
        self.s_core = s + 1 - 2 * self.core
        self.s_y = lax.rem(s + ns // 2, ns)

    def s_at_z(self, z):
        return (self.ylo * self.nz + lax.rem(z + self.nz, self.nz)) * 2 + self.core

    def tile_at(self, d):
        return lax.rem(self.t + d + self.nt, self.nt)


def remote(src, dst, send, recv, s, t):
    return pltpu.make_async_remote_copy(
        src_ref=src, dst_ref=dst, send_sem=send, recv_sem=recv,
        device_id={"scan": s, "tile": t}, device_id_type=MESH,
    )


def greet(peers):
    barrier = pltpu.get_barrier_semaphore()
    for s, t in peers:
        pl.semaphore_signal(barrier, inc=1, device_id={"scan": s, "tile": t}, device_id_type=MESH)
    pl.semaphore_wait(barrier, len(peers))


PARTS = 4


def gather_stage(at, nt, spec_ref, probe_ref, ext_ref, full_ref, sems, meanwhile):
    loc_sem, xs, xr, ps, pr, zs, zr, qs, qr, cs, cr = sems
    height = spec_ref.shape[1]
    prow, n = probe_ref.shape[1:]
    step = height // PARTS
    c, z = at.core, at.z
    part = lax.rem(z, PARTS)
    steps = [1, -1, 2, -2]
    groups = [c, 2 + c]
    first, last = at.t == 0, at.t == nt - 1

    def lower(g, lo, size):
        return ext_ref.at[groups[g], pl.ds(pl.multiple_of(height + part * step + lo, 8), size), :]

    def source(g):
        return spec_ref.at[groups[g], pl.ds(pl.multiple_of(part * step, 8), step), :]

    strips = [remote(source(g), lower(g, 0, step), xs.at[g], xr.at[g], at.s, at.tile_at(-1)) for g in range(2)]
    fillers = [pltpu.make_async_copy(source(g), lower(g, 0, step), loc_sem.at[1 + g]) for g in range(2)]
    plane = 4 * c + part
    mine = pl.ds(pl.multiple_of(at.t * prow, prow), prow)
    probes = [
        remote(probe_ref.at[plane], full_ref.at[plane, mine, :], ps.at[d], pr.at[d], at.s, at.tile_at(d))
        for d in range(1, nt)
    ]
    own_probe = pltpu.make_async_copy(probe_ref.at[plane], full_ref.at[plane, mine, :], loc_sem.at[0])

    def send(g):
        pl.when(jnp.logical_not(first))(strips[g].start)
        pl.when(last)(fillers[g].start)

    def arrived(g):
        pl.when(jnp.logical_not(last))(strips[g].wait_recv)
        pl.when(last)(fillers[g].wait)

    send(0)
    for copy in probes:
        copy.start()
    own_probe.start()
    send(1)
    meanwhile()

    half = n // 2
    cuts = [(0, step), (0, step), (0, step // 2), (step // 2, step // 2)]
    spans = [pl.ds(0, n), pl.ds(0, n), pl.ds(0, half), pl.ds(half, half)]
    strip_z = [
        [
            remote(lower(g, *cuts[k]), lower(g, *cuts[k]), zs.at[g, k], zr.at[g, k], at.s_at_z(z + steps[k]), at.t)
            for k in range(4)
        ]
        for g in range(2)
    ]
    probe_z = [
        remote(full_ref.at[plane, spans[k], :], full_ref.at[plane, spans[k], :], qs.at[k], qr.at[k],
               at.s_at_z(z + steps[k]), at.t)
        for k in range(4)
    ]
    whole = [ext_ref.at[groups[g], pl.ds(height, height), :] for g in range(2)]
    whole += [full_ref.at[pl.ds(4 * c, 4)]]
    shares = [remote(whole[k], whole[k], cs.at[k], cr.at[k], at.s_core, at.t) for k in range(3)]

    arrived(0)
    for copy in strip_z[0]:
        copy.start()
    own_probe.wait()
    for copy in probes:
        copy.wait_recv()
    for copy in probe_z:
        copy.start()
    for copy in strip_z[0]:
        copy.wait_recv()
    shares[0].start()
    arrived(1)
    for copy in strip_z[1]:
        copy.start()
    for copy in probe_z:
        copy.wait_recv()
    shares[2].start()
    shares[0].wait_recv()
    shares[2].wait_recv()

    def share_later():
        for copy in strip_z[1]:
            copy.wait_recv()
        shares[1].start()

    def finish():
        shares[1].wait_recv()
        for strip in strips:
            pl.when(jnp.logical_not(first))(strip.wait_send)
        for copy in probes + strip_z[0] + strip_z[1] + probe_z + shares:
            copy.wait_send()

    return share_later, finish


def put_right(ref, m, n, part, value):
    high = value.astype(BF16)
    low = (value - high.astype(F32)).astype(BF16)
    rows = pl.ds(m * n, n)
    ref[rows, pl.ds(part * n, n)] = high
    ref[rows, pl.ds((2 + part) * n, n)] = low
    ref[rows, pl.ds((4 + part) * n, n)] = high


def put_left(ref, m, n, part, value):
    high = value.astype(BF16)
    low = (value - high.astype(F32)).astype(BF16)
    cols = pl.ds(m * n, n)
    ref[pl.ds(part * n, n), cols] = high
    ref[pl.ds((2 + part) * n, n), cols] = low
    ref[pl.ds((4 + part) * n, n), cols] = high


def split_rows(source, parts, first, rows, planes):
    for p in planes:
        value = source[p]
        high = value.astype(BF16)
        parts[2 * p, pl.ds(first, rows)] = high
        parts[2 * p + 1, pl.ds(first, rows)] = (value - high.astype(F32)).astype(BF16)


def select(condition):
    return jnp.where(condition, 1.0, 0.0).astype(BF16)


def window_stage(owner, off_ref, ext_ref, probe_ref, meas_ref, right_ref, left_ref, kern_ref,
                 canvas_ref, pgrad_ref, xa, xb, ya, yb, patch, wave, parts, cut, got, grads, tall, spread,
                 share_later, finish):
    planes, height2, width = ext_ref.shape
    height = height2 // 2
    n = probe_ref.shape[1]
    modes = probe_ref.shape[0] // 2
    per_group = off_ref.shape[1]
    batch = [(slot, m) for slot in range(CAP) for m in range(modes)]

    def dot(a, b):
        return jnp.dot(a, b, preferred_element_type=F32)

    def mul_right(src, inverse):
        return dot(src[...], right_ref[inverse])

    def mul_left(src, inverse):
        return dot(left_ref[inverse], src[...])

    def right_parts(out, b):
        rows = out[b * n:(b + 1) * n]
        return rows[:, :n], rows[:, n:]

    def left_parts(out, b):
        cols = out[:, b * n:(b + 1) * n]
        return cols[:n], cols[n:]

    def right_to_left(src, dst, inverse):
        out = mul_right(src, inverse)
        for b in range(len(batch)):
            re, im = right_parts(out, b)
            put_left(dst, b, n, 0, re)
            put_left(dst, b, n, 1, im)

    def left_to_right(src, dst, inverse):
        out = mul_left(src, inverse)
        for b in range(len(batch)):
            re, im = left_parts(out, b)
            put_right(dst, b, n, 0, re)
            put_right(dst, b, n, 1, im)

    def through_kernel(src, dst, sign):
        out = mul_left(src, 0)
        kre, kim = kern_ref[0], kern_ref[1] * sign
        for b in range(len(batch)):
            re, im = left_parts(out, b)
            put_left(dst, b, n, 0, re * kre - im * kim)
            put_left(dst, b, n, 1, re * kim + im * kre)

    hits, corners = [], []
    for slot in range(CAP):
        rank = jnp.int32(0)
        row = jnp.int32(4 * height2)
        col = jnp.int32(0)
        chosen = []
        for b in range(per_group):
            here = ((off_ref[0, b] // height) == owner).astype(jnp.int32)
            hit = here * (rank == slot).astype(jnp.int32)
            row = row + hit * (off_ref[0, b] - owner * height - 4 * height2)
            col = col + hit * off_ref[1, b]
            chosen.append(hit.astype(F32))
            rank = rank + here
        hits.append(chosen)
        corners.append((row, col))

    def iotas(*shape):
        return [lax.broadcasted_iota(jnp.int32, shape, axis) for axis in range(2)]

    i, j = iotas(width, n)
    for slot, (row, col) in enumerate(corners):
        cut[:, pl.ds(slot * n, n)] = select(i == j + col)

    def cut_windows(k):
        split_rows(ext_ref.at[:, pl.ds(height, height), :], parts, height, height, (2 * k, 2 * k + 1))
        out = dot(parts[pl.ds(4 * k, 4)].reshape(4 * height2, width), cut[...])
        for q in range(2):
            for part in range(2):
                rows = out[(2 * q + part) * height2:(2 * q + part + 1) * height2]
                for slot in range(CAP):
                    lanes = pl.ds((2 * k + q) * n, n)
                    got[slot, pl.ds(part * height2, height2), lanes] = rows[:, slot * n:(slot + 1) * n].astype(BF16)
        i, j = iotas(n, height2)
        for slot, (row, _) in enumerate(corners):
            pick = select(j == i + row)
            out = dot(jnp.concatenate([pick, pick], 1), got[slot, :, pl.ds(2 * k * n, 2 * n)])
            for q in range(2):
                patch[slot, 2 * k + q] = out[:, q * n:(q + 1) * n]

    cut_windows(0)
    for b, (slot, m) in enumerate(batch):
        pre, pim = probe_ref[2 * m], probe_ref[2 * m + 1]
        put_right(xa, b, n, 0, pre * patch[slot, 0] - pim * patch[slot, 1])
        put_right(xa, b, n, 1, pre * patch[slot, 1] + pim * patch[slot, 0])
    right_to_left(xa, ya, 0)
    through_kernel(ya, yb, 1.0)
    share_later()
    left_to_right(yb, xb, 1)
    finish()
    cut_windows(1)
    out = mul_right(xb, 1)
    for b, (slot, m) in enumerate(batch):
        re, im = right_parts(out, b)
        wave[b, 0] = re
        wave[b, 1] = im
        put_right(xa, b, n, 0, re * patch[slot, 2] - im * patch[slot, 3])
        put_right(xa, b, n, 1, re * patch[slot, 3] + im * patch[slot, 2])
    right_to_left(xa, ya, 0)
    out = mul_left(ya, 0)
    for slot in range(CAP):
        weight = sum(hits[slot])
        measured = hits[slot][0] * meas_ref[0]
        for b in range(1, per_group):
            measured = measured + hits[slot][b] * meas_ref[b]
        model = jnp.zeros((n, n), F32)
        for m in range(modes):
            re, im = left_parts(out, slot * modes + m)
            model = model + re * re + im * im
        twice = (2.0 * weight) * (model - measured)
        for m in range(modes):
            b = slot * modes + m
            re, im = left_parts(out, b)
            put_left(yb, b, n, 0, twice * re)
            put_left(yb, b, n, 1, twice * im)
    left_to_right(yb, xb, 1)
    out = mul_right(xb, 1)

    def pad_window(slot, p, grad):
        high = grad.astype(BF16)
        grads[slot, :, pl.ds(2 * p * n, n)] = high
        grads[slot, :, pl.ds((2 * p + 1) * n, n)] = (grad - high.astype(F32)).astype(BF16)

    for slot in range(CAP):
        gre = jnp.zeros((n, n), F32)
        gim = jnp.zeros((n, n), F32)
        for m in range(modes):
            b = slot * modes + m
            re, im = right_parts(out, b)
            wre, wim = wave[b, 0], wave[b, 1]
            gre = gre + wre * re + wim * im
            gim = gim + wre * im - wim * re
            put_right(xa, b, n, 0, patch[slot, 2] * re + patch[slot, 3] * im)
            put_right(xa, b, n, 1, patch[slot, 2] * im - patch[slot, 3] * re)
        pad_window(slot, 2, gre)
        pad_window(slot, 3, gim)
    right_to_left(xa, ya, 0)
    through_kernel(ya, yb, -1.0)
    left_to_right(yb, xb, 1)
    out = mul_right(xb, 1)
    for m in range(modes):
        pgre = jnp.zeros((n, n), F32)
        pgim = jnp.zeros((n, n), F32)
        for slot in range(CAP):
            re, im = right_parts(out, slot * modes + m)
            pgre = pgre + patch[slot, 0] * re + patch[slot, 1] * im
            pgim = pgim + patch[slot, 0] * im - patch[slot, 1] * re
        pgrad_ref[m, 0] = pgre
        pgrad_ref[m, 1] = pgim
    for slot in range(CAP):
        hre = jnp.zeros((n, n), F32)
        him = jnp.zeros((n, n), F32)
        for m in range(modes):
            re, im = right_parts(out, slot * modes + m)
            pre, pim = probe_ref[2 * m], probe_ref[2 * m + 1]
            hre = hre + pre * re + pim * im
            him = him + pre * im - pim * re
        pad_window(slot, 0, hre)
        pad_window(slot, 1, him)

    i, j = iotas(height2, n)
    u, v = iotas(n, width)
    for slot, (row, col) in enumerate(corners):
        out = dot(select(i == j + row), grads[slot])
        for p in range(planes):
            for part in range(2):
                piece = out[:, (2 * p + part) * n:(2 * p + part + 1) * n]
                tall[pl.ds(p * height2, height2), pl.ds((2 * slot + part) * n, n)] = piece.astype(BF16)
        put = select(v == u + col)
        spread[pl.ds(2 * slot * n, n), :] = put
        spread[pl.ds((2 * slot + 1) * n, n), :] = put
    canvas_ref[...] = dot(tall[...], spread[...]).reshape(canvas_ref.shape)


STREAMS = tuple((k, 1) for k in range(5))


OWN = 7


def sum_stage(at, nt, canvas, pgrad, gbuf, bufs, sems):
    got_c, got_p, pacc, first, upbuf, dnbuf, mine, pmine, ybuf, rimbuf, tbuf = bufs
    cs, cr, us, ur, ds_, dr, ms, mr, ts, tr, gs, gr, ks, kr = sems
    nz = at.nz
    half = nz // 2
    core, z = at.core, at.z
    own2 = pl.ds(2 * core, 2)
    other2 = pl.ds(2 - 2 * core, 2)
    lanes = 128
    def chunk(i):
        return lax.rem(i + 2 * nz, nz)

    order = [half]
    for k in range(half - 1, 0, -1):
        order += [-k, k]
    order += [0]

    def swap_at(k):
        i = order.index(k)
        return remote(canvas.at[other2, :, chunk(z + k)], got_c.at[:, :, chunk(z + k)], cs.at[i], cr.at[i], at.s_core, at.t)

    swap_p = remote(pgrad.at[other2], got_p, cs.at[nz], cr.at[nz], at.s_core, at.t)
    swaps = [swap_at(k) for k in order]
    for copy in swaps[:2] + [swap_p] + swaps[2:]:
        copy.start()

    def probe_rows():
        swap_p.wait_recv()
        for m in range(2):
            for ri in range(2):
                whole = pgrad[2 * core + m, ri] + got_p[m, ri]
                for r in range(4):
                    j = (2 * m + ri) * 4 + r
                    for t in range(nt):
                        piece = whole[16 * t + 4 * r:16 * t + 4 * r + 4]
                        pacc[j, pl.ds(4 * (t % 2), 4), pl.ds(lanes * (t // 2), lanes)] = piece

    def local(k, idx):
        j = chunk(z + k)
        if idx == 4:
            return pacc[j]
        return canvas[2 * core + idx % 2, idx // 2, j] + got_c[idx % 2, idx // 2, j]

    def up(i, p):
        part = pl.ds(*STREAMS[p])
        src = first.at[0, part] if i == 0 else upbuf.at[i - 1, part]
        return remote(src, upbuf.at[i, part], us.at[i, p], ur.at[i, p], at.s_at_z(z + 1), at.t)

    def down(i, p):
        part = pl.ds(*STREAMS[p])
        src = first.at[1, part] if i == 0 else dnbuf.at[i - 1, part]
        return remote(src, dnbuf.at[i, part], ds_.at[i, p], dr.at[i, p], at.s_at_z(z - 1), at.t)

    count = len(STREAMS)
    for k, r, start in ((half, 0, up), (1 - half, 1, down)):
        swap_at(k).wait_recv()
        for p in range(4):
            first[r, p] = local(k, p)
            start(0, p).start()
    probe_rows()
    for k, r, start in ((half, 0, up), (1 - half, 1, down)):
        first[r, 4] = local(k, 4)
        start(0, 4).start()
    for i in range(half):
        ku, kd = half - 1 - i, 2 + i - half
        if i < half - 1:
            swap_at(ku).wait_recv()
        if i < half - 2:
            swap_at(kd).wait_recv()
        for p in range(count):
            span = range(STREAMS[p][0], STREAMS[p][0] + STREAMS[p][1])
            up(i, p).wait_recv()
            if i < half - 1:
                for idx in span:
                    upbuf[i, idx] += local(ku, idx)
                up(i + 1, p).start()
                down(i, p).wait_recv()
            if i < half - 2:
                for idx in span:
                    dnbuf[i, idx] += local(kd, idx)
                down(i + 1, p).start()
    swap_at(0).wait_recv()
    for idx in range(5):
        mine[idx] = local(0, idx) + upbuf[half - 1, idx] + dnbuf[half - 2, idx]
    for q in range(nt // 2):
        pmine[q] = mine[4, :, lanes * q:lanes * (q + 1)]

    to_y = remote(mine.at[pl.ds(0, 2)], ybuf, ms.at[0], mr.at[0], at.s_y, at.t)
    rim_a = remote(mine.at[pl.ds(2, 2)], rimbuf.at[0], ms.at[1], mr.at[1], at.s, at.tile_at(1))
    rim_b = remote(mine.at[pl.ds(2, 2)], rimbuf.at[1], ms.at[2], mr.at[2], at.s_y, at.tile_at(1))
    tiles = [
        remote(pmine.at[at.tile_at(d) // 2], tbuf.at[at.ylo, at.t], ts.at[e, d], tr.at[e, d], s, at.tile_at(d))
        for e, s in ((0, at.s), (1, at.s_y)) for d in range(e ^ 1, nt)
    ]
    rim_b.start()
    rim_a.start()
    to_y.start()
    for copy in tiles:
        copy.start()
    tbuf[at.ylo, at.t] = pmine[at.t // 2]
    to_y.wait_recv()
    rim_a.wait_recv()
    rim_b.wait_recv()
    for k in range(2):
        final = (mine[k] + ybuf[k]) + (rimbuf[0, k] + rimbuf[1, k])
        for l in range(4):
            gbuf[core, OWN, 4 * k + l] = final[:, lanes * l:lanes * (l + 1)]
    for copy in tiles:
        copy.wait_recv()
    total = tbuf[0, 0]
    for k in range(1, 2 * nt):
        total = total + tbuf[k // nt, k % nt]
    gbuf[core, OWN, 8] = jnp.where(lax.rem(at.t, 2) == 1, pltpu.roll(total, 4, 0), total)

    def pass_on(i, k, to, part=slice(0, 9)):
        new = k - to + 16 * (k - to < -OWN)
        part = pl.ds(part.start, part.stop - part.start)
        return remote(gbuf.at[core, k + OWN, part], gbuf.at[core, new + OWN, part], gs.at[i], gr.at[i], at.s_at_z(z + to), at.t)

    def share(k, lo, hi):
        part = gbuf.at[core, pl.ds(lo + OWN, hi - lo + 1)]
        return remote(part, part, ks.at[k], kr.at[k], at.s_core, at.t)

    top, low = slice(0, 4), slice(4, 9)
    far = [pass_on(0, 0, 6), pass_on(1, 0, -6)]
    near = [pass_on(2, 0, 1), pass_on(3, 0, -1), pass_on(4, 0, 2), pass_on(5, 0, -2)]
    after_near = [pass_on(6, 2, -1), pass_on(7, 2, -2), pass_on(8, -2, 1), pass_on(9, -2, 2)]
    after_far = [
        pass_on(10, 6, -1), pass_on(11, 6, 1), pass_on(12, 6, -2, top),
        pass_on(13, -6, 1), pass_on(14, -6, -1), pass_on(15, -6, 2, low),
    ]
    shares = [share(0, -2, 2), share(1, 3, 4), share(2, -4, -3), share(3, 5, 8), share(4, -7, -5)]
    for copy in far + near:
        copy.start()
    near[3].wait_recv()
    near[2].wait_recv()
    near[1].wait_recv()
    near[0].wait_recv()
    for copy in after_near:
        copy.start()
    far[0].wait_recv()
    far[1].wait_recv()
    for copy in after_far:
        copy.start()
    shares[0].start()
    for copy in after_near:
        copy.wait_recv()
    shares[1].start()
    shares[2].start()
    for copy in after_far:
        copy.wait_recv()
    shares[3].start()
    shares[4].start()
    for copy in shares:
        copy.wait_recv()

    for copy in [swap_p, to_y, rim_a, rim_b] + swaps + tiles + far + near + after_near + after_far + shares:
        copy.wait_send()
    for p in range(count):
        for i in range(half):
            up(i, p).wait_send()
        for i in range(half - 1):
            down(i, p).wait_send()


def fused_kernel(ns, nt, off, spec, probe, meas_hbm, right_hbm, left_hbm, kern_hbm, gbuf, *scratch):
    ext, full, meas, right, left, kern, canvas, pgrad, xa, xb, ya, yb, patch, wave = scratch[:14]
    selecting, bufs, sems = scratch[14:20], scratch[20:31], scratch[31:]
    loads = [
        pltpu.make_async_copy(src, dst, sems[0].at[k])
        for k, (src, dst) in enumerate([(meas_hbm, meas), (right_hbm, right), (left_hbm, left), (kern_hbm, kern)])
    ]
    for copy in loads:
        copy.start()
    at = Place(ns, nt)
    z = at.z
    greet(
        [(s, at.tile_at(d)) for s in (at.s, at.s_y) for d in range(1, nt)]
        + [(at.s_at_z(z + d), at.t) for d in (1, -1, 2, -2, 6, -6)] + [(at.s_y, at.t), (at.s_core, at.t)]
    )

    def split_own():
        split_rows(spec, selecting[0], 0, spec.shape[1], range(spec.shape[0]))

    later = gather_stage(at, nt, spec, probe, ext, full, sems[1:12], split_own)
    for copy in loads:
        copy.wait()
    window_stage(at.t, off, ext, full, meas, right, left, kern, canvas, pgrad, xa, xb, ya, yb, patch, wave, *selecting, *later)
    sum_stage(at, nt, canvas, pgrad, gbuf, bufs, sems[12:])


def place_kernel(ns, nt, gbuf, out, pout):
    z = Place(ns, nt).z
    nz = gbuf.shape[1]
    lanes = gbuf.shape[4]
    for j in range(nz):
        slot = lax.rem(j - z + OWN + nz, nz)
        for c in range(2):
            for k in range(2):
                for l in range(4):
                    out[2 * c + k, j, :, lanes * l:lanes * (l + 1)] = gbuf[c, slot, 4 * k + l]
            m, ri, r = j // 8, (j // 4) % 2, j % 4
            pout[2 * c + m, ri, pl.ds(4 * r, 4), :] = gbuf[c, slot, 8, 0:4]


def shards(ns, nt, specimen, probe_modes, offsets, intensity):
    slices, two, height, width = specimen.shape
    modes, _, prow, n = probe_modes.shape
    planes = slices * two
    nz = ns // 4
    half = nz // 2
    sub = height // nz
    count = len(STREAMS)
    right, left, kernel = dft_tables(n)
    dma = pltpu.SemaphoreType.DMA
    vmem = pl.BlockSpec(memory_space=pltpu.VMEM)
    hbm = pl.BlockSpec(memory_space=pl.ANY)

    def f32(*shape):
        return pltpu.VMEM(shape, F32)

    def pair(*shape):
        return [dma(shape), dma(shape)]

    gathered = pl.pallas_call(
        partial(fused_kernel, ns, nt),
        name="gradient_sums",
        out_shape=jax.ShapeDtypeStruct((2, nz, 9, 8, n), F32),
        in_specs=[pl.BlockSpec(memory_space=pltpu.SMEM), vmem, vmem] + [hbm] * 4,
        out_specs=vmem,
        scratch_shapes=[
            f32(planes, 2 * height, width),
            f32(modes * two, n, n),
            f32(*intensity.shape),
            pltpu.VMEM(right.shape, BF16),
            pltpu.VMEM(left.shape, BF16),
            f32(2, n, n),
            f32(planes, 2, nz, sub, width),
            f32(modes, two, n, n),
            pltpu.VMEM((CAP * modes * n, 6 * n), BF16),
            pltpu.VMEM((CAP * modes * n, 6 * n), BF16),
            pltpu.VMEM((6 * n, CAP * modes * n), BF16),
            pltpu.VMEM((6 * n, CAP * modes * n), BF16),
            f32(CAP, planes, n, n),
            f32(CAP * modes, 2, n, n),
            pltpu.VMEM((2 * planes, 2 * height, width), BF16),
            pltpu.VMEM((width, CAP * n), BF16),
            pltpu.VMEM((CAP, 4 * height, planes * n), BF16),
            pltpu.VMEM((CAP, n, 2 * planes * n), BF16),
            pltpu.VMEM((planes * 2 * height, 2 * CAP * n), BF16),
            pltpu.VMEM((2 * CAP * n, width), BF16),
            f32(2, 2, nz, sub, width),
            f32(2, two, n, n),
            f32(nz, sub, width),
            f32(2, 5, sub, width),
            f32(half, 5, sub, width),
            f32(half - 1, 5, sub, width),
            f32(5, sub, width),
            f32(nt // 2, 8, n),
            f32(2, sub, width),
            f32(2, 2, sub, width),
            f32(2, nt, 8, n),
        ]
        + [dma((4,))]
        + [dma((3,))] + pair(2) + pair(nt) + pair(2, 4) + pair(4) + pair(3)
        + pair(nz + 1) + pair(half, count) + pair(half - 1, count) + pair(3) + pair(2, nt) + pair(16) + pair(5),
        compiler_params=pltpu.CompilerParams(collective_id=0, has_side_effects=True, vmem_limit_bytes=VMEM_LIMIT),
    )(
        offsets, specimen.reshape(planes, height, width), probe_modes.reshape(modes * two, prow, n), intensity,
        jnp.asarray(right), jnp.asarray(left), jnp.asarray(kernel),
    )
    out, pout = pl.pallas_call(
        partial(place_kernel, ns, nt),
        name="place_rows",
        out_shape=(
            jax.ShapeDtypeStruct((planes, nz, sub, width), F32),
            jax.ShapeDtypeStruct((modes, two, prow, n), F32),
        ),
        in_specs=[vmem],
        out_specs=[vmem] * 2,
        compiler_params=pltpu.CompilerParams(vmem_limit_bytes=VMEM_LIMIT),
    )(gathered)
    return out.reshape(specimen.shape), pout


def solution(mesh):
    ns, nt = mesh.shape["scan"], mesh.shape["tile"]
    return jax.shard_map(
        partial(shards, ns, nt),
        mesh=mesh,
        in_specs=(
            P(None, None, "tile", None),
            P(None, None, "tile", None),
            P(None, "scan"),
            P("scan", None, None),
        ),
        out_specs=(P(None, None, "tile", None), P(None, None, "tile", None)),
        check_vma=False,
    )
```

```python
from functools import partial
import math

import jax
import jax.numpy as jnp
import numpy as np
from jax import lax
from jax.experimental import pallas as pl
from jax.experimental.pallas import tpu as pltpu
from jax.sharding import PartitionSpec as P

fresnel_phase = 40.0
F32 = jnp.float32
BF16 = jnp.bfloat16
MESH = pl.DeviceIdType.MESH
VMEM_LIMIT = 56 * 1024 * 1024
CAP = 2


def split_bf16(table):
    high = table.astype(BF16)
    low = (table - high.astype(np.float64)).astype(BF16)
    return np.asarray(high), np.asarray(low)


def dft_tables(n):
    k = np.arange(n)
    angle = (np.outer(k, k) % n) * (-2.0 * np.pi / n)
    re, im = np.cos(angle) / math.sqrt(n), np.sin(angle) / math.sqrt(n)
    forward = np.block([[re, im], [-im, re]])
    inverse = np.block([[re, -im], [im, re]])
    fh, fl = split_bf16(forward)
    ih, il = split_bf16(inverse)
    right = np.stack([np.concatenate([fh, fh, fl], 0), np.concatenate([ih, ih, il], 0)])
    left = np.stack([np.concatenate([ih, ih, il], 1), np.concatenate([fh, fh, fl], 1)])
    freq = np.fft.fftfreq(n)
    phi = -fresnel_phase * (freq[:, None] ** 2 + freq[None, :] ** 2)
    kernel = np.stack([np.cos(phi), np.sin(phi)]).astype(np.float32)
    return right, left, kernel


class Place:
    def __init__(self, ns, nt):
        self.ns, self.nt, self.nz = ns, nt, ns // 4
        s, t = lax.axis_index("scan"), lax.axis_index("tile")
        self.s, self.t = s, t
        self.core = lax.rem(s, 2)
        self.z = lax.rem(s // 2, self.nz)
        self.ylo = s // (2 * self.nz)
        self.s_core = s + 1 - 2 * self.core
        self.s_y = lax.rem(s + ns // 2, ns)

    def s_at_z(self, z):
        return (self.ylo * self.nz + lax.rem(z + self.nz, self.nz)) * 2 + self.core

    def tile_at(self, d):
        return lax.rem(self.t + d + self.nt, self.nt)


def remote(src, dst, send, recv, s, t):
    return pltpu.make_async_remote_copy(
        src_ref=src, dst_ref=dst, send_sem=send, recv_sem=recv,
        device_id={"scan": s, "tile": t}, device_id_type=MESH,
    )


def greet(peers):
    barrier = pltpu.get_barrier_semaphore()
    for s, t in peers:
        pl.semaphore_signal(barrier, inc=1, device_id={"scan": s, "tile": t}, device_id_type=MESH)
    pl.semaphore_wait(barrier, len(peers))


PARTS = 4


def gather_stage(at, nt, spec_ref, probe_ref, ext_ref, full_ref, sems, meanwhile):
    loc_sem, xs, xr, ps, pr, zs, zr, qs, qr, cs, cr = sems
    height = spec_ref.shape[1]
    prow, n = probe_ref.shape[1:]
    step = height // PARTS
    c, z = at.core, at.z
    part = lax.rem(z, PARTS)
    steps = [1, -1, 2, -2]
    groups = [c, 2 + c]
    first, last = at.t == 0, at.t == nt - 1

    def lower(g, lo, size):
        return ext_ref.at[groups[g], pl.ds(pl.multiple_of(height + part * step + lo, 8), size), :]

    def source(g):
        return spec_ref.at[groups[g], pl.ds(pl.multiple_of(part * step, 8), step), :]

    strips = [remote(source(g), lower(g, 0, step), xs.at[g], xr.at[g], at.s, at.tile_at(-1)) for g in range(2)]
    fillers = [pltpu.make_async_copy(source(g), lower(g, 0, step), loc_sem.at[1 + g]) for g in range(2)]
    plane = 4 * c + part
    mine = pl.ds(pl.multiple_of(at.t * prow, prow), prow)
    probes = [
        remote(probe_ref.at[plane], full_ref.at[plane, mine, :], ps.at[d], pr.at[d], at.s, at.tile_at(d))
        for d in range(1, nt)
    ]
    own_probe = pltpu.make_async_copy(probe_ref.at[plane], full_ref.at[plane, mine, :], loc_sem.at[0])

    def send(g):
        pl.when(jnp.logical_not(first))(strips[g].start)
        pl.when(last)(fillers[g].start)

    def arrived(g):
        pl.when(jnp.logical_not(last))(strips[g].wait_recv)
        pl.when(last)(fillers[g].wait)

    send(0)
    for copy in probes:
        copy.start()
    own_probe.start()
    send(1)
    meanwhile()

    half = n // 2
    cuts = [(0, step), (0, step), (0, step // 2), (step // 2, step // 2)]
    spans = [pl.ds(0, n), pl.ds(0, n), pl.ds(0, half), pl.ds(half, half)]
    strip_z = [
        [
            remote(lower(g, *cuts[k]), lower(g, *cuts[k]), zs.at[g, k], zr.at[g, k], at.s_at_z(z + steps[k]), at.t)
            for k in range(4)
        ]
        for g in range(2)
    ]
    probe_z = [
        remote(full_ref.at[plane, spans[k], :], full_ref.at[plane, spans[k], :], qs.at[k], qr.at[k],
               at.s_at_z(z + steps[k]), at.t)
        for k in range(4)
    ]
    whole = [ext_ref.at[groups[g], pl.ds(height, height), :] for g in range(2)]
    whole += [full_ref.at[pl.ds(4 * c, 4)]]
    shares = [remote(whole[k], whole[k], cs.at[k], cr.at[k], at.s_core, at.t) for k in range(3)]

    arrived(0)
    for copy in strip_z[0]:
        copy.start()
    own_probe.wait()
    for copy in probes:
        copy.wait_recv()
    for copy in probe_z:
        copy.start()
    for copy in strip_z[0]:
        copy.wait_recv()
    shares[0].start()
    arrived(1)
    for copy in strip_z[1]:
        copy.start()
    for copy in probe_z:
        copy.wait_recv()
    shares[2].start()
    shares[0].wait_recv()
    shares[2].wait_recv()

    def share_later():
        for copy in strip_z[1]:
            copy.wait_recv()
        shares[1].start()

    def finish():
        shares[1].wait_recv()

    def drain():
        for strip in strips:
            pl.when(jnp.logical_not(first))(strip.wait_send)
        for copy in probes + strip_z[0] + strip_z[1] + probe_z + shares:
            copy.wait_send()

    return share_later, finish, drain


def put_right(ref, m, n, part, value):
    high = value.astype(BF16)
    low = (value - high.astype(F32)).astype(BF16)
    rows = pl.ds(m * n, n)
    ref[rows, pl.ds(part * n, n)] = high
    ref[rows, pl.ds((2 + part) * n, n)] = low
    ref[rows, pl.ds((4 + part) * n, n)] = high


def put_left(ref, m, n, part, value):
    high = value.astype(BF16)
    low = (value - high.astype(F32)).astype(BF16)
    cols = pl.ds(m * n, n)
    ref[pl.ds(part * n, n), cols] = high
    ref[pl.ds((2 + part) * n, n), cols] = low
    ref[pl.ds((4 + part) * n, n), cols] = high


def split_rows(source, parts, first, rows, planes):
    for p in planes:
        value = source[p]
        high = value.astype(BF16)
        parts[2 * p, pl.ds(first, rows)] = high
        parts[2 * p + 1, pl.ds(first, rows)] = (value - high.astype(F32)).astype(BF16)


def select(condition):
    return jnp.where(condition, 1.0, 0.0).astype(BF16)


def window_stage(owner, off_ref, ext_ref, probe_ref, meas_ref, right_ref, left_ref, kern_ref,
                 canvas_ref, pgrad_ref, xa, xb, ya, yb, patch, wave, parts, cut, got, grads, tall, spread,
                 share_later, finish):
    planes, height2, width = ext_ref.shape
    height = height2 // 2
    n = probe_ref.shape[1]
    modes = probe_ref.shape[0] // 2
    per_group = off_ref.shape[1]
    batch = [(slot, m) for slot in range(CAP) for m in range(modes)]

    def dot(a, b):
        return jnp.dot(a, b, preferred_element_type=F32)

    def mul_right(src, inverse):
        return dot(src[...], right_ref[inverse])

    def mul_left(src, inverse):
        return dot(left_ref[inverse], src[...])

    def right_parts(out, b):
        rows = out[b * n:(b + 1) * n]
        return rows[:, :n], rows[:, n:]

    def left_parts(out, b):
        cols = out[:, b * n:(b + 1) * n]
        return cols[:n], cols[n:]

    def right_to_left(src, dst, inverse):
        out = mul_right(src, inverse)
        for b in range(len(batch)):
            re, im = right_parts(out, b)
            put_left(dst, b, n, 0, re)
            put_left(dst, b, n, 1, im)

    def left_to_right(src, dst, inverse):
        out = mul_left(src, inverse)
        for b in range(len(batch)):
            re, im = left_parts(out, b)
            put_right(dst, b, n, 0, re)
            put_right(dst, b, n, 1, im)

    def through_kernel(src, dst, sign):
        out = mul_left(src, 0)
        kre, kim = kern_ref[0], kern_ref[1] * sign
        for b in range(len(batch)):
            re, im = left_parts(out, b)
            put_left(dst, b, n, 0, re * kre - im * kim)
            put_left(dst, b, n, 1, re * kim + im * kre)

    hits, corners = [], []
    for slot in range(CAP):
        rank = jnp.int32(0)
        row = jnp.int32(4 * height2)
        col = jnp.int32(0)
        chosen = []
        for b in range(per_group):
            here = ((off_ref[0, b] // height) == owner).astype(jnp.int32)
            hit = here * (rank == slot).astype(jnp.int32)
            row = row + hit * (off_ref[0, b] - owner * height - 4 * height2)
            col = col + hit * off_ref[1, b]
            chosen.append(hit.astype(F32))
            rank = rank + here
        hits.append(chosen)
        corners.append((row, col))

    def iotas(*shape):
        return [lax.broadcasted_iota(jnp.int32, shape, axis) for axis in range(2)]

    i, j = iotas(width, n)
    for slot, (row, col) in enumerate(corners):
        cut[:, pl.ds(slot * n, n)] = select(i == j + col)

    def cut_windows(k):
        split_rows(ext_ref.at[:, pl.ds(height, height), :], parts, height, height, (2 * k, 2 * k + 1))
        out = dot(parts[pl.ds(4 * k, 4)].reshape(4 * height2, width), cut[...])
        for q in range(2):
            for part in range(2):
                rows = out[(2 * q + part) * height2:(2 * q + part + 1) * height2]
                for slot in range(CAP):
                    lanes = pl.ds((2 * k + q) * n, n)
                    got[slot, pl.ds(part * height2, height2), lanes] = rows[:, slot * n:(slot + 1) * n].astype(BF16)
        i, j = iotas(n, height2)
        for slot, (row, _) in enumerate(corners):
            pick = select(j == i + row)
            out = dot(jnp.concatenate([pick, pick], 1), got[slot, :, pl.ds(2 * k * n, 2 * n)])
            for q in range(2):
                patch[slot, 2 * k + q] = out[:, q * n:(q + 1) * n]

    cut_windows(0)
    for b, (slot, m) in enumerate(batch):
        pre, pim = probe_ref[2 * m], probe_ref[2 * m + 1]
        put_right(xa, b, n, 0, pre * patch[slot, 0] - pim * patch[slot, 1])
        put_right(xa, b, n, 1, pre * patch[slot, 1] + pim * patch[slot, 0])
    right_to_left(xa, ya, 0)
    through_kernel(ya, yb, 1.0)
    share_later()
    left_to_right(yb, xb, 1)
    finish()
    cut_windows(1)
    out = mul_right(xb, 1)
    for b, (slot, m) in enumerate(batch):
        re, im = right_parts(out, b)
        wave[b, 0] = re
        wave[b, 1] = im
        put_right(xa, b, n, 0, re * patch[slot, 2] - im * patch[slot, 3])
        put_right(xa, b, n, 1, re * patch[slot, 3] + im * patch[slot, 2])
    right_to_left(xa, ya, 0)
    out = mul_left(ya, 0)
    for slot in range(CAP):
        weight = sum(hits[slot])
        measured = hits[slot][0] * meas_ref[0]
        for b in range(1, per_group):
            measured = measured + hits[slot][b] * meas_ref[b]
        model = jnp.zeros((n, n), F32)
        for m in range(modes):
            re, im = left_parts(out, slot * modes + m)
            model = model + re * re + im * im
        twice = (2.0 * weight) * (model - measured)
        for m in range(modes):
            b = slot * modes + m
            re, im = left_parts(out, b)
            put_left(yb, b, n, 0, twice * re)
            put_left(yb, b, n, 1, twice * im)
    left_to_right(yb, xb, 1)
    out = mul_right(xb, 1)

    def pad_window(slot, p, grad):
        high = grad.astype(BF16)
        grads[slot, :, pl.ds(2 * p * n, n)] = high
        grads[slot, :, pl.ds((2 * p + 1) * n, n)] = (grad - high.astype(F32)).astype(BF16)

    for slot in range(CAP):
        gre = jnp.zeros((n, n), F32)
        gim = jnp.zeros((n, n), F32)
        for m in range(modes):
            b = slot * modes + m
            re, im = right_parts(out, b)
            wre, wim = wave[b, 0], wave[b, 1]
            gre = gre + wre * re + wim * im
            gim = gim + wre * im - wim * re
            put_right(xa, b, n, 0, patch[slot, 2] * re + patch[slot, 3] * im)
            put_right(xa, b, n, 1, patch[slot, 2] * im - patch[slot, 3] * re)
        pad_window(slot, 2, gre)
        pad_window(slot, 3, gim)
    right_to_left(xa, ya, 0)
    through_kernel(ya, yb, -1.0)
    left_to_right(yb, xb, 1)
    out = mul_right(xb, 1)
    for m in range(modes):
        pgre = jnp.zeros((n, n), F32)
        pgim = jnp.zeros((n, n), F32)
        for slot in range(CAP):
            re, im = right_parts(out, slot * modes + m)
            pgre = pgre + patch[slot, 0] * re + patch[slot, 1] * im
            pgim = pgim + patch[slot, 0] * im - patch[slot, 1] * re
        pgrad_ref[m, 0] = pgre
        pgrad_ref[m, 1] = pgim
    for slot in range(CAP):
        hre = jnp.zeros((n, n), F32)
        him = jnp.zeros((n, n), F32)
        for m in range(modes):
            re, im = right_parts(out, slot * modes + m)
            pre, pim = probe_ref[2 * m], probe_ref[2 * m + 1]
            hre = hre + pre * re + pim * im
            him = him + pre * im - pim * re
        pad_window(slot, 0, hre)
        pad_window(slot, 1, him)

    i, j = iotas(height2, n)
    u, v = iotas(n, width)
    for slot, (row, col) in enumerate(corners):
        out = dot(select(i == j + row), grads[slot])
        for p in range(planes):
            for part in range(2):
                piece = out[:, (2 * p + part) * n:(2 * p + part + 1) * n]
                tall[pl.ds(p * height2, height2), pl.ds((2 * slot + part) * n, n)] = piece.astype(BF16)
        put = select(v == u + col)
        spread[pl.ds(2 * slot * n, n), :] = put
        spread[pl.ds((2 * slot + 1) * n, n), :] = put
    canvas_ref[...] = dot(tall[...], spread[...]).reshape(canvas_ref.shape)


STREAMS = ((0, 2), (2, 2), (4, 1))
AHEAD = 2


OWN = 7


def sum_stage(at, nt, canvas, pgrad, gbuf, bufs, sems, drain):
    got_c, got_p, pacc, first, upbuf, dnbuf, mine, pmine, ybuf, rimbuf, tbuf = bufs
    cs, cr, us, ur, ds_, dr, ms, mr, ts, tr, gs, gr, ks, kr = sems
    nz = at.nz
    half = nz // 2
    core, z = at.core, at.z
    own2 = pl.ds(2 * core, 2)
    other2 = pl.ds(2 - 2 * core, 2)
    lanes = 128
    def chunk(i):
        return lax.rem(i + 2 * nz, nz)

    order = [half]
    for k in range(half - 1, 0, -1):
        order += [-k, k]
    order += [0]

    def swap_at(k):
        i = order.index(k)
        return remote(canvas.at[other2, :, chunk(z + k)], got_c.at[:, :, chunk(z + k)], cs.at[i], cr.at[i], at.s_core, at.t)

    swap_p = remote(pgrad.at[other2], got_p, cs.at[nz], cr.at[nz], at.s_core, at.t)
    swaps = [swap_at(k) for k in order]
    early = 2 + 2 * AHEAD
    for copy in swaps[:2] + [swap_p] + swaps[2:early]:
        copy.start()

    def probe_rows():
        swap_p.wait_recv()
        for m in range(2):
            for ri in range(2):
                whole = pgrad[2 * core + m, ri] + got_p[m, ri]
                for r in range(4):
                    j = (2 * m + ri) * 4 + r
                    for t in range(nt):
                        piece = whole[16 * t + 4 * r:16 * t + 4 * r + 4]
                        pacc[j, pl.ds(4 * (t % 2), 4), pl.ds(lanes * (t // 2), lanes)] = piece

    def local(k, idx):
        j = chunk(z + k)
        if idx == 4:
            return pacc[j]
        return canvas[2 * core + idx % 2, idx // 2, j] + got_c[idx % 2, idx // 2, j]

    def up(i, p):
        part = pl.ds(*STREAMS[p])
        src = first.at[0, part] if i == 0 else upbuf.at[i - 1, part]
        return remote(src, upbuf.at[i, part], us.at[i, p], ur.at[i, p], at.s_at_z(z + 1), at.t)

    def down(i, p):
        part = pl.ds(*STREAMS[p])
        src = first.at[1, part] if i == 0 else dnbuf.at[i - 1, part]
        return remote(src, dnbuf.at[i, part], ds_.at[i, p], dr.at[i, p], at.s_at_z(z - 1), at.t)

    count = len(STREAMS)
    for k, r, start in ((half, 0, up), (1 - half, 1, down)):
        swap_at(k).wait_recv()
        for p in range(count - 1):
            for idx in range(STREAMS[p][0], STREAMS[p][0] + STREAMS[p][1]):
                first[r, idx] = local(k, idx)
            start(0, p).start()
    probe_rows()
    for k, r, start in ((half, 0, up), (1 - half, 1, down)):
        first[r, 4] = local(k, 4)
        start(0, count - 1).start()
    for i in range(half):
        ku, kd = half - 1 - i, 2 + i - half
        for copy in swaps[early + 2 * i:early + 2 * i + 2]:
            copy.start()
        if i < half - 1:
            swap_at(ku).wait_recv()
        if i < half - 2:
            swap_at(kd).wait_recv()
        for p in range(count):
            span = range(STREAMS[p][0], STREAMS[p][0] + STREAMS[p][1])
            up(i, p).wait_recv()
            if i < half - 1:
                for idx in span:
                    upbuf[i, idx] += local(ku, idx)
                up(i + 1, p).start()
                down(i, p).wait_recv()
            if i < half - 2:
                for idx in span:
                    dnbuf[i, idx] += local(kd, idx)
                down(i + 1, p).start()
    swap_at(0).wait_recv()
    for idx in range(5):
        mine[idx] = local(0, idx) + upbuf[half - 1, idx] + dnbuf[half - 2, idx]
    for q in range(nt // 2):
        pmine[q] = mine[4, :, lanes * q:lanes * (q + 1)]

    to_y = remote(mine.at[pl.ds(0, 2)], ybuf, ms.at[0], mr.at[0], at.s_y, at.t)
    rim_a = remote(mine.at[pl.ds(2, 2)], rimbuf.at[0], ms.at[1], mr.at[1], at.s, at.tile_at(1))
    rim_b = remote(mine.at[pl.ds(2, 2)], rimbuf.at[1], ms.at[2], mr.at[2], at.s_y, at.tile_at(1))
    tiles = [
        remote(pmine.at[at.tile_at(d) // 2], tbuf.at[at.ylo, at.t], ts.at[e, d], tr.at[e, d], s, at.tile_at(d))
        for e, s in ((0, at.s), (1, at.s_y)) for d in range(e ^ 1, nt)
    ]
    rim_b.start()
    rim_a.start()
    to_y.start()
    for copy in tiles:
        copy.start()
    tbuf[at.ylo, at.t] = pmine[at.t // 2]
    to_y.wait_recv()
    rim_a.wait_recv()
    rim_b.wait_recv()
    for k in range(2):
        final = (mine[k] + ybuf[k]) + (rimbuf[0, k] + rimbuf[1, k])
        for l in range(4):
            gbuf[core, OWN, 4 * k + l] = final[:, lanes * l:lanes * (l + 1)]
    for copy in tiles:
        copy.wait_recv()
    total = tbuf[0, 0]
    for k in range(1, 2 * nt):
        total = total + tbuf[k // nt, k % nt]
    gbuf[core, OWN, 8] = jnp.where(lax.rem(at.t, 2) == 1, pltpu.roll(total, 4, 0), total)

    def pass_on(i, k, to, part=slice(0, 9)):
        new = k - to + 16 * (k - to < -OWN)
        part = pl.ds(part.start, part.stop - part.start)
        return remote(gbuf.at[core, k + OWN, part], gbuf.at[core, new + OWN, part], gs.at[i], gr.at[i], at.s_at_z(z + to), at.t)

    def share(k, lo, hi):
        part = gbuf.at[core, pl.ds(lo + OWN, hi - lo + 1)]
        return remote(part, part, ks.at[k], kr.at[k], at.s_core, at.t)

    top, low = slice(0, 4), slice(4, 9)
    far = [pass_on(0, 0, 6), pass_on(1, 0, -6)]
    near = [pass_on(2, 0, 1), pass_on(3, 0, -1), pass_on(4, 0, 2), pass_on(5, 0, -2)]
    after_near = [pass_on(6, 2, -1), pass_on(7, 2, -2), pass_on(8, -2, 1), pass_on(9, -2, 2)]
    after_far = [
        pass_on(10, 6, -1), pass_on(11, 6, 1), pass_on(12, 6, -2, top),
        pass_on(13, -6, 1), pass_on(14, -6, -1), pass_on(15, -6, 2, low),
    ]
    shares = [share(0, -2, 2), share(1, 3, 4), share(2, -4, -3), share(3, 5, 8), share(4, -7, -5)]
    for copy in far + near:
        copy.start()
    drain()
    for copy in [swap_p, to_y, rim_a, rim_b] + swaps + tiles:
        copy.wait_send()
    for p in range(count):
        for i in range(half):
            up(i, p).wait_send()
        for i in range(half - 1):
            down(i, p).wait_send()
    near[3].wait_recv()
    near[2].wait_recv()
    near[1].wait_recv()
    near[0].wait_recv()
    for copy in after_near:
        copy.start()
    far[0].wait_recv()
    far[1].wait_recv()
    for copy in after_far:
        copy.start()
    shares[0].start()
    for copy in after_near:
        copy.wait_recv()
    shares[1].start()
    shares[2].start()
    for copy in after_far:
        copy.wait_recv()
    shares[3].start()
    shares[4].start()
    for copy in shares:
        copy.wait_recv()

    for copy in far + near + after_near + after_far + shares:
        copy.wait_send()


def fused_kernel(ns, nt, off, spec, probe, meas_hbm, right_hbm, left_hbm, kern_hbm, gbuf, *scratch):
    ext, full, meas, right, left, kern, canvas, pgrad, xa, xb, ya, yb, patch, wave = scratch[:14]
    selecting, bufs, sems = scratch[14:20], scratch[20:31], scratch[31:]
    loads = [
        pltpu.make_async_copy(src, dst, sems[0].at[k])
        for k, (src, dst) in enumerate([(meas_hbm, meas), (right_hbm, right), (left_hbm, left), (kern_hbm, kern)])
    ]
    for copy in loads:
        copy.start()
    at = Place(ns, nt)
    z = at.z
    greet(
        [(s, at.tile_at(d)) for s in (at.s, at.s_y) for d in range(1, nt)]
        + [(at.s_at_z(z + d), at.t) for d in (1, -1, 2, -2, 6, -6)] + [(at.s_y, at.t), (at.s_core, at.t)]
    )

    def split_own():
        split_rows(spec, selecting[0], 0, spec.shape[1], range(spec.shape[0]))

    share_later, finish, drain = gather_stage(at, nt, spec, probe, ext, full, sems[1:12], split_own)
    for copy in loads:
        copy.wait()
    window_stage(at.t, off, ext, full, meas, right, left, kern, canvas, pgrad, xa, xb, ya, yb, patch, wave, *selecting,
                 share_later, finish)
    sum_stage(at, nt, canvas, pgrad, gbuf, bufs, sems[12:], drain)


def place_kernel(ns, nt, gbuf, out, pout):
    z = Place(ns, nt).z
    nz = gbuf.shape[1]
    lanes = gbuf.shape[4]
    for j in range(nz):
        slot = lax.rem(j - z + OWN + nz, nz)
        for c in range(2):
            for k in range(2):
                for l in range(4):
                    out[2 * c + k, j, :, lanes * l:lanes * (l + 1)] = gbuf[c, slot, 4 * k + l]
            m, ri, r = j // 8, (j // 4) % 2, j % 4
            pout[2 * c + m, ri, pl.ds(4 * r, 4), :] = gbuf[c, slot, 8, 0:4]


def shards(ns, nt, specimen, probe_modes, offsets, intensity):
    slices, two, height, width = specimen.shape
    modes, _, prow, n = probe_modes.shape
    planes = slices * two
    nz = ns // 4
    half = nz // 2
    sub = height // nz
    count = len(STREAMS)
    right, left, kernel = dft_tables(n)
    dma = pltpu.SemaphoreType.DMA
    vmem = pl.BlockSpec(memory_space=pltpu.VMEM)
    hbm = pl.BlockSpec(memory_space=pl.ANY)

    def f32(*shape):
        return pltpu.VMEM(shape, F32)

    def pair(*shape):
        return [dma(shape), dma(shape)]

    gathered = pl.pallas_call(
        partial(fused_kernel, ns, nt),
        name="gradient_sums",
        out_shape=jax.ShapeDtypeStruct((2, nz, 9, 8, n), F32),
        in_specs=[pl.BlockSpec(memory_space=pltpu.SMEM), vmem, vmem] + [hbm] * 4,
        out_specs=vmem,
        scratch_shapes=[
            f32(planes, 2 * height, width),
            f32(modes * two, n, n),
            f32(*intensity.shape),
            pltpu.VMEM(right.shape, BF16),
            pltpu.VMEM(left.shape, BF16),
            f32(2, n, n),
            f32(planes, 2, nz, sub, width),
            f32(modes, two, n, n),
            pltpu.VMEM((CAP * modes * n, 6 * n), BF16),
            pltpu.VMEM((CAP * modes * n, 6 * n), BF16),
            pltpu.VMEM((6 * n, CAP * modes * n), BF16),
            pltpu.VMEM((6 * n, CAP * modes * n), BF16),
            f32(CAP, planes, n, n),
            f32(CAP * modes, 2, n, n),
            pltpu.VMEM((2 * planes, 2 * height, width), BF16),
            pltpu.VMEM((width, CAP * n), BF16),
            pltpu.VMEM((CAP, 4 * height, planes * n), BF16),
            pltpu.VMEM((CAP, n, 2 * planes * n), BF16),
            pltpu.VMEM((planes * 2 * height, 2 * CAP * n), BF16),
            pltpu.VMEM((2 * CAP * n, width), BF16),
            f32(2, 2, nz, sub, width),
            f32(2, two, n, n),
            f32(nz, sub, width),
            f32(2, 5, sub, width),
            f32(half, 5, sub, width),
            f32(half - 1, 5, sub, width),
            f32(5, sub, width),
            f32(nt // 2, 8, n),
            f32(2, sub, width),
            f32(2, 2, sub, width),
            f32(2, nt, 8, n),
        ]
        + [dma((4,))]
        + [dma((3,))] + pair(2) + pair(nt) + pair(2, 4) + pair(4) + pair(3)
        + pair(nz + 1) + pair(half, count) + pair(half - 1, count) + pair(3) + pair(2, nt) + pair(16) + pair(5),
        compiler_params=pltpu.CompilerParams(collective_id=0, has_side_effects=True, vmem_limit_bytes=VMEM_LIMIT),
    )(
        offsets, specimen.reshape(planes, height, width), probe_modes.reshape(modes * two, prow, n), intensity,
        jnp.asarray(right), jnp.asarray(left), jnp.asarray(kernel),
    )
    out, pout = pl.pallas_call(
        partial(place_kernel, ns, nt),
        name="place_rows",
        out_shape=(
            jax.ShapeDtypeStruct((planes, nz, sub, width), F32),
            jax.ShapeDtypeStruct((modes, two, prow, n), F32),
        ),
        in_specs=[vmem],
        out_specs=[vmem] * 2,
        compiler_params=pltpu.CompilerParams(vmem_limit_bytes=VMEM_LIMIT),
    )(gathered)
    return out.reshape(specimen.shape), pout


def solution(mesh):
    ns, nt = mesh.shape["scan"], mesh.shape["tile"]
    return jax.shard_map(
        partial(shards, ns, nt),
        mesh=mesh,
        in_specs=(
            P(None, None, "tile", None),
            P(None, None, "tile", None),
            P(None, "scan"),
            P("scan", None, None),
        ),
        out_specs=(P(None, None, "tile", None), P(None, None, "tile", None)),
        check_vma=False,
    )
```

```python
from functools import partial
import math

import jax
import jax.numpy as jnp
import numpy as np
from jax import lax
from jax.experimental import pallas as pl
from jax.experimental.pallas import tpu as pltpu
from jax.sharding import PartitionSpec as P

fresnel_phase = 40.0
F32 = jnp.float32
BF16 = jnp.bfloat16
MESH = pl.DeviceIdType.MESH
VMEM_LIMIT = 56 * 1024 * 1024
CAP = 2


def split_bf16(table):
    high = table.astype(BF16)
    low = (table - high.astype(np.float64)).astype(BF16)
    return np.asarray(high), np.asarray(low)


def dft_tables(n):
    k = np.arange(n)
    angle = (np.outer(k, k) % n) * (-2.0 * np.pi / n)
    re, im = np.cos(angle) / math.sqrt(n), np.sin(angle) / math.sqrt(n)
    forward = np.block([[re, im], [-im, re]])
    inverse = np.block([[re, -im], [im, re]])
    fh, fl = split_bf16(forward)
    ih, il = split_bf16(inverse)
    right = np.stack([np.concatenate([fh, fh, fl], 0), np.concatenate([ih, ih, il], 0)])
    left = np.stack([np.concatenate([ih, ih, il], 1), np.concatenate([fh, fh, fl], 1)])
    freq = np.fft.fftfreq(n)
    phi = -fresnel_phase * (freq[:, None] ** 2 + freq[None, :] ** 2)
    kernel = np.stack([np.cos(phi), np.sin(phi)]).astype(np.float32)
    return right, left, kernel


class Place:
    def __init__(self, ns, nt):
        self.ns, self.nt, self.nz = ns, nt, ns // 4
        s, t = lax.axis_index("scan"), lax.axis_index("tile")
        self.s, self.t = s, t
        self.core = lax.rem(s, 2)
        self.z = lax.rem(s // 2, self.nz)
        self.ylo = s // (2 * self.nz)
        self.s_core = s + 1 - 2 * self.core
        self.s_y = lax.rem(s + ns // 2, ns)

    def s_at_z(self, z):
        return (self.ylo * self.nz + lax.rem(z + self.nz, self.nz)) * 2 + self.core

    def tile_at(self, d):
        return lax.rem(self.t + d + self.nt, self.nt)


def remote(src, dst, send, recv, s, t):
    return pltpu.make_async_remote_copy(
        src_ref=src, dst_ref=dst, send_sem=send, recv_sem=recv,
        device_id={"scan": s, "tile": t}, device_id_type=MESH,
    )


def greet(peers):
    barrier = pltpu.get_barrier_semaphore()
    for s, t in peers:
        pl.semaphore_signal(barrier, inc=1, device_id={"scan": s, "tile": t}, device_id_type=MESH)
    pl.semaphore_wait(barrier, len(peers))


PARTS = 4


def gather_stage(at, nt, spec_ref, probe_ref, ext_ref, full_ref, sems, meanwhile):
    loc_sem, xs, xr, ps, pr, zs, zr, cs, cr = sems
    height = spec_ref.shape[1]
    prow, n = probe_ref.shape[1:]
    step = height // PARTS
    c, z = at.core, at.z
    part = lax.rem(z, PARTS)
    steps = [1, -1, 2, -2]
    groups = [c, 2 + c]
    first, last = at.t == 0, at.t == nt - 1

    def lower(g, lo, size):
        return ext_ref.at[groups[g], pl.ds(pl.multiple_of(height + part * step + lo, 8), size), :]

    def source(g):
        return spec_ref.at[groups[g], pl.ds(pl.multiple_of(part * step, 8), step), :]

    strips = [remote(source(g), lower(g, 0, step), xs.at[g], xr.at[g], at.s, at.tile_at(-1)) for g in range(2)]
    fillers = [pltpu.make_async_copy(source(g), lower(g, 0, step), loc_sem.at[1 + g]) for g in range(2)]
    four = pl.ds(4 * c, 4)
    mine = pl.ds(pl.multiple_of(at.t * prow, prow), prow)
    probes = [
        remote(probe_ref.at[four], full_ref.at[four, mine, :], ps.at[d], pr.at[d], at.s, at.tile_at(d))
        for d in range(1, nt)
    ]
    own_probe = pltpu.make_async_copy(probe_ref.at[four], full_ref.at[four, mine, :], loc_sem.at[0])

    def send(g):
        pl.when(jnp.logical_not(first))(strips[g].start)
        pl.when(last)(fillers[g].start)

    def arrived(g):
        pl.when(jnp.logical_not(last))(strips[g].wait_recv)
        pl.when(last)(fillers[g].wait)

    send(0)
    for copy in probes:
        copy.start()
    own_probe.start()
    send(1)
    meanwhile()

    cuts = [(0, step), (0, step), (0, step // 2), (step // 2, step // 2)]
    strip_z = [
        [
            remote(lower(g, *cuts[k]), lower(g, *cuts[k]), zs.at[g, k], zr.at[g, k], at.s_at_z(z + steps[k]), at.t)
            for k in range(4)
        ]
        for g in range(2)
    ]
    whole = [ext_ref.at[groups[g], pl.ds(height, height), :] for g in range(2)]
    whole += [full_ref.at[four]]
    shares = [remote(whole[k], whole[k], cs.at[k], cr.at[k], at.s_core, at.t) for k in range(3)]

    arrived(0)
    for copy in strip_z[0]:
        copy.start()
    arrived(1)
    for copy in strip_z[1]:
        copy.start()
    own_probe.wait()
    for copy in probes:
        copy.wait_recv()
    shares[2].start()
    for copy in strip_z[0]:
        copy.wait_recv()
    shares[0].start()
    shares[0].wait_recv()
    shares[2].wait_recv()

    def share_later():
        for copy in strip_z[1]:
            copy.wait_recv()
        shares[1].start()

    def finish():
        shares[1].wait_recv()

    def drain():
        for strip in strips:
            pl.when(jnp.logical_not(first))(strip.wait_send)
        for copy in probes + strip_z[0] + strip_z[1] + shares:
            copy.wait_send()

    return share_later, finish, drain


def put_right(ref, m, n, part, value):
    high = value.astype(BF16)
    low = (value - high.astype(F32)).astype(BF16)
    rows = pl.ds(m * n, n)
    ref[rows, pl.ds(part * n, n)] = high
    ref[rows, pl.ds((2 + part) * n, n)] = low
    ref[rows, pl.ds((4 + part) * n, n)] = high


def put_left(ref, m, n, part, value):
    high = value.astype(BF16)
    low = (value - high.astype(F32)).astype(BF16)
    cols = pl.ds(m * n, n)
    ref[pl.ds(part * n, n), cols] = high
    ref[pl.ds((2 + part) * n, n), cols] = low
    ref[pl.ds((4 + part) * n, n), cols] = high


def split_rows(source, parts, first, rows, planes):
    for p in planes:
        value = source[p]
        high = value.astype(BF16)
        parts[2 * p, pl.ds(first, rows)] = high
        parts[2 * p + 1, pl.ds(first, rows)] = (value - high.astype(F32)).astype(BF16)


def select(condition):
    return jnp.where(condition, 1.0, 0.0).astype(BF16)


def window_stage(owner, off_ref, ext_ref, probe_ref, meas_ref, right_ref, left_ref, kern_ref,
                 canvas_ref, pgrad_ref, xa, xb, ya, yb, patch, wave, parts, cut, got, grads, tall, spread,
                 share_later, finish):
    planes, height2, width = ext_ref.shape
    height = height2 // 2
    n = probe_ref.shape[1]
    modes = probe_ref.shape[0] // 2
    per_group = off_ref.shape[1]
    batch = [(slot, m) for slot in range(CAP) for m in range(modes)]

    def dot(a, b):
        return jnp.dot(a, b, preferred_element_type=F32)

    def mul_right(src, inverse):
        return dot(src[...], right_ref[inverse])

    def mul_left(src, inverse):
        return dot(left_ref[inverse], src[...])

    def right_parts(out, b):
        rows = out[b * n:(b + 1) * n]
        return rows[:, :n], rows[:, n:]

    def left_parts(out, b):
        cols = out[:, b * n:(b + 1) * n]
        return cols[:n], cols[n:]

    def right_to_left(src, dst, inverse):
        out = mul_right(src, inverse)
        for b in range(len(batch)):
            re, im = right_parts(out, b)
            put_left(dst, b, n, 0, re)
            put_left(dst, b, n, 1, im)

    def left_to_right(src, dst, inverse):
        out = mul_left(src, inverse)
        for b in range(len(batch)):
            re, im = left_parts(out, b)
            put_right(dst, b, n, 0, re)
            put_right(dst, b, n, 1, im)

    def through_kernel(src, dst, sign):
        out = mul_left(src, 0)
        kre, kim = kern_ref[0], kern_ref[1] * sign
        for b in range(len(batch)):
            re, im = left_parts(out, b)
            put_left(dst, b, n, 0, re * kre - im * kim)
            put_left(dst, b, n, 1, re * kim + im * kre)

    hits, corners = [], []
    for slot in range(CAP):
        rank = jnp.int32(0)
        row = jnp.int32(4 * height2)
        col = jnp.int32(0)
        chosen = []
        for b in range(per_group):
            here = ((off_ref[0, b] // height) == owner).astype(jnp.int32)
            hit = here * (rank == slot).astype(jnp.int32)
            row = row + hit * (off_ref[0, b] - owner * height - 4 * height2)
            col = col + hit * off_ref[1, b]
            chosen.append(hit.astype(F32))
            rank = rank + here
        hits.append(chosen)
        corners.append((row, col))

    def iotas(*shape):
        return [lax.broadcasted_iota(jnp.int32, shape, axis) for axis in range(2)]

    i, j = iotas(width, n)
    for slot, (row, col) in enumerate(corners):
        cut[:, pl.ds(slot * n, n)] = select(i == j + col)

    def cut_windows(k):
        split_rows(ext_ref.at[:, pl.ds(height, height), :], parts, height, height, (2 * k, 2 * k + 1))
        out = dot(parts[pl.ds(4 * k, 4)].reshape(4 * height2, width), cut[...])
        for q in range(2):
            for part in range(2):
                rows = out[(2 * q + part) * height2:(2 * q + part + 1) * height2]
                for slot in range(CAP):
                    lanes = pl.ds((2 * k + q) * n, n)
                    got[slot, pl.ds(part * height2, height2), lanes] = rows[:, slot * n:(slot + 1) * n].astype(BF16)
        i, j = iotas(n, height2)
        for slot, (row, _) in enumerate(corners):
            pick = select(j == i + row)
            out = dot(jnp.concatenate([pick, pick], 1), got[slot, :, pl.ds(2 * k * n, 2 * n)])
            for q in range(2):
                patch[slot, 2 * k + q] = out[:, q * n:(q + 1) * n]

    cut_windows(0)
    for b, (slot, m) in enumerate(batch):
        pre, pim = probe_ref[2 * m], probe_ref[2 * m + 1]
        put_right(xa, b, n, 0, pre * patch[slot, 0] - pim * patch[slot, 1])
        put_right(xa, b, n, 1, pre * patch[slot, 1] + pim * patch[slot, 0])
    right_to_left(xa, ya, 0)
    through_kernel(ya, yb, 1.0)
    share_later()
    left_to_right(yb, xb, 1)
    finish()
    cut_windows(1)
    out = mul_right(xb, 1)
    for b, (slot, m) in enumerate(batch):
        re, im = right_parts(out, b)
        wave[b, 0] = re
        wave[b, 1] = im
        put_right(xa, b, n, 0, re * patch[slot, 2] - im * patch[slot, 3])
        put_right(xa, b, n, 1, re * patch[slot, 3] + im * patch[slot, 2])
    right_to_left(xa, ya, 0)
    out = mul_left(ya, 0)
    for slot in range(CAP):
        weight = sum(hits[slot])
        measured = hits[slot][0] * meas_ref[0]
        for b in range(1, per_group):
            measured = measured + hits[slot][b] * meas_ref[b]
        model = jnp.zeros((n, n), F32)
        for m in range(modes):
            re, im = left_parts(out, slot * modes + m)
            model = model + re * re + im * im
        twice = (2.0 * weight) * (model - measured)
        for m in range(modes):
            b = slot * modes + m
            re, im = left_parts(out, b)
            put_left(yb, b, n, 0, twice * re)
            put_left(yb, b, n, 1, twice * im)
    left_to_right(yb, xb, 1)
    out = mul_right(xb, 1)

    def pad_window(slot, p, grad):
        high = grad.astype(BF16)
        grads[slot, :, pl.ds(2 * p * n, n)] = high
        grads[slot, :, pl.ds((2 * p + 1) * n, n)] = (grad - high.astype(F32)).astype(BF16)

    for slot in range(CAP):
        gre = jnp.zeros((n, n), F32)
        gim = jnp.zeros((n, n), F32)
        for m in range(modes):
            b = slot * modes + m
            re, im = right_parts(out, b)
            wre, wim = wave[b, 0], wave[b, 1]
            gre = gre + wre * re + wim * im
            gim = gim + wre * im - wim * re
            put_right(xa, b, n, 0, patch[slot, 2] * re + patch[slot, 3] * im)
            put_right(xa, b, n, 1, patch[slot, 2] * im - patch[slot, 3] * re)
        pad_window(slot, 2, gre)
        pad_window(slot, 3, gim)
    right_to_left(xa, ya, 0)
    through_kernel(ya, yb, -1.0)
    left_to_right(yb, xb, 1)
    out = mul_right(xb, 1)
    for m in range(modes):
        pgre = jnp.zeros((n, n), F32)
        pgim = jnp.zeros((n, n), F32)
        for slot in range(CAP):
            re, im = right_parts(out, slot * modes + m)
            pgre = pgre + patch[slot, 0] * re + patch[slot, 1] * im
            pgim = pgim + patch[slot, 0] * im - patch[slot, 1] * re
        pgrad_ref[m, 0] = pgre
        pgrad_ref[m, 1] = pgim
    for slot in range(CAP):
        hre = jnp.zeros((n, n), F32)
        him = jnp.zeros((n, n), F32)
        for m in range(modes):
            re, im = right_parts(out, slot * modes + m)
            pre, pim = probe_ref[2 * m], probe_ref[2 * m + 1]
            hre = hre + pre * re + pim * im
            him = him + pre * im - pim * re
        pad_window(slot, 0, hre)
        pad_window(slot, 1, him)

    i, j = iotas(height2, n)
    u, v = iotas(n, width)
    for slot, (row, col) in enumerate(corners):
        out = dot(select(i == j + row), grads[slot])
        for p in range(planes):
            for part in range(2):
                piece = out[:, (2 * p + part) * n:(2 * p + part + 1) * n]
                tall[pl.ds(p * height2, height2), pl.ds((2 * slot + part) * n, n)] = piece.astype(BF16)
        put = select(v == u + col)
        spread[pl.ds(2 * slot * n, n), :] = put
        spread[pl.ds((2 * slot + 1) * n, n), :] = put
    canvas_ref[...] = dot(tall[...], spread[...]).reshape(canvas_ref.shape)


STREAMS = ((0, 2), (2, 2), (4, 1))


OWN = 7


def sum_stage(at, nt, canvas, pgrad, gbuf, bufs, sems, drain):
    got_c, got_p, pacc, first, chain, mine, pmine, ybuf, rimbuf, tbuf = bufs
    cs, cr, us, ur, ms, mr, ts, tr, gs, gr, ks, kr = sems
    nz = at.nz
    core, z = at.core, at.z
    own2 = pl.ds(2 * core, 2)
    other2 = pl.ds(2 - 2 * core, 2)
    lanes = 128
    def chunk(i):
        return lax.rem(i + 2 * nz, nz)

    order = [8, -7, 4, -4, 7, -6, 3, -3, 6, -5, 2, -2, 5, 1, -1, 0]

    def swap_at(k):
        i = order.index(k)
        return remote(canvas.at[other2, :, chunk(z + k)], got_c.at[:, :, chunk(z + k)], cs.at[i], cr.at[i], at.s_core, at.t)

    swap_p = remote(pgrad.at[other2], got_p, cs.at[nz], cr.at[nz], at.s_core, at.t)
    swaps = [swap_at(k) for k in order]
    for copy in swaps[:4] + [swap_p] + swaps[4:8]:
        copy.start()

    def probe_rows():
        swap_p.wait_recv()
        for m in range(2):
            for ri in range(2):
                whole = pgrad[2 * core + m, ri] + got_p[m, ri]
                for r in range(4):
                    j = (2 * m + ri) * 4 + r
                    for t in range(nt):
                        piece = whole[16 * t + 4 * r:16 * t + 4 * r + 4]
                        pacc[j, pl.ds(4 * (t % 2), 4), pl.ds(lanes * (t // 2), lanes)] = piece

    def local(k, idx):
        j = chunk(z + k)
        if idx == 4:
            return pacc[j]
        return canvas[2 * core + idx % 2, idx // 2, j] + got_c[idx % 2, idx // 2, j]

    chains = [(8, 1, 4, True), (-7, -1, 3, True), (4, 1, 4, False), (-4, -1, 4, False)]
    count = len(STREAMS)

    def target(q, i):
        return chains[q][0] - i * chains[q][1]

    def hop(q, i, p):
        _, way, hops, jumps = chains[q]
        part = pl.ds(*STREAMS[p])
        src = first.at[q, part] if i == 0 else chain.at[q, i - 1, part]
        to = target(q, i) if jumps and i == hops - 1 else way
        return remote(src, chain.at[q, i, part], us.at[q, i, p], ur.at[q, i, p], at.s_at_z(z + to), at.t)

    def span(p):
        return range(STREAMS[p][0], STREAMS[p][0] + STREAMS[p][1])

    for q in range(4):
        swap_at(target(q, 0)).wait_recv()
        for p in range(count - 1):
            for idx in span(p):
                first[q, idx] = local(target(q, 0), idx)
            hop(q, 0, p).start()
    probe_rows()
    for q in range(4):
        first[q, 4] = local(target(q, 0), 4)
        hop(q, 0, count - 1).start()
    for i in range(4):
        for copy in swaps[8 + 4 * i:12 + 4 * i]:
            copy.start()
        for q in range(4):
            if i + 1 < chains[q][2]:
                swap_at(target(q, i + 1)).wait_recv()
        for p in range(count):
            for q in range(4):
                if i < chains[q][2]:
                    hop(q, i, p).wait_recv()
                if i + 1 < chains[q][2]:
                    for idx in span(p):
                        chain[q, i, idx] += local(target(q, i + 1), idx)
                    hop(q, i + 1, p).start()
    swap_at(0).wait_recv()
    for idx in range(5):
        total = local(0, idx)
        for q in range(4):
            total = total + chain[q, chains[q][2] - 1, idx]
        mine[idx] = total
    for q in range(nt // 2):
        pmine[q] = mine[4, :, lanes * q:lanes * (q + 1)]

    to_y = remote(mine.at[pl.ds(0, 2)], ybuf, ms.at[0], mr.at[0], at.s_y, at.t)
    rim_a = remote(mine.at[pl.ds(2, 2)], rimbuf.at[0], ms.at[1], mr.at[1], at.s, at.tile_at(1))
    rim_b = remote(mine.at[pl.ds(2, 2)], rimbuf.at[1], ms.at[2], mr.at[2], at.s_y, at.tile_at(1))
    tiles = [
        remote(pmine.at[at.tile_at(d) // 2], tbuf.at[at.ylo, at.t], ts.at[e, d], tr.at[e, d], s, at.tile_at(d))
        for e, s in ((0, at.s), (1, at.s_y)) for d in range(e ^ 1, nt)
    ]
    rim_b.start()
    rim_a.start()
    to_y.start()
    for copy in tiles:
        copy.start()
    tbuf[at.ylo, at.t] = pmine[at.t // 2]
    to_y.wait_recv()
    rim_a.wait_recv()
    rim_b.wait_recv()
    for k in range(2):
        final = (mine[k] + ybuf[k]) + (rimbuf[0, k] + rimbuf[1, k])
        for l in range(4):
            gbuf[core, OWN, 4 * k + l] = final[:, lanes * l:lanes * (l + 1)]
    for copy in tiles:
        copy.wait_recv()
    total = tbuf[0, 0]
    for k in range(1, 2 * nt):
        total = total + tbuf[k // nt, k % nt]
    gbuf[core, OWN, 8] = jnp.where(lax.rem(at.t, 2) == 1, pltpu.roll(total, 4, 0), total)

    def pass_on(i, k, to, part=slice(0, 9)):
        new = k - to + 16 * (k - to < -OWN)
        part = pl.ds(part.start, part.stop - part.start)
        return remote(gbuf.at[core, k + OWN, part], gbuf.at[core, new + OWN, part], gs.at[i], gr.at[i], at.s_at_z(z + to), at.t)

    def share(k, lo, hi):
        part = gbuf.at[core, pl.ds(lo + OWN, hi - lo + 1)]
        return remote(part, part, ks.at[k], kr.at[k], at.s_core, at.t)

    top, low = slice(0, 4), slice(4, 9)
    far = [pass_on(0, 0, 6), pass_on(1, 0, -6)]
    near = [pass_on(2, 0, 1), pass_on(3, 0, -1), pass_on(4, 0, 2), pass_on(5, 0, -2)]
    after_near = [pass_on(6, 2, -1), pass_on(7, 2, -2), pass_on(8, -2, 1), pass_on(9, -2, 2)]
    after_far = [
        pass_on(10, 6, -1), pass_on(11, 6, 1), pass_on(12, 6, -2, top),
        pass_on(13, -6, 1), pass_on(14, -6, -1), pass_on(15, -6, 2, low),
    ]
    shares = [share(0, -2, 2), share(1, 3, 4), share(2, -4, -3), share(3, 5, 8), share(4, -7, -5)]
    for copy in far + near:
        copy.start()
    drain()
    for copy in [swap_p, to_y, rim_a, rim_b] + swaps + tiles:
        copy.wait_send()
    for q in range(4):
        for i in range(chains[q][2]):
            for p in range(count):
                hop(q, i, p).wait_send()
    near[3].wait_recv()
    near[2].wait_recv()
    near[1].wait_recv()
    near[0].wait_recv()
    for copy in after_near:
        copy.start()
    far[0].wait_recv()
    far[1].wait_recv()
    for copy in after_far:
        copy.start()
    shares[0].start()
    for copy in after_near:
        copy.wait_recv()
    shares[1].start()
    shares[2].start()
    for copy in after_far:
        copy.wait_recv()
    shares[3].start()
    shares[4].start()
    for copy in shares:
        copy.wait_recv()

    for copy in far + near + after_near + after_far + shares:
        copy.wait_send()


def fused_kernel(ns, nt, off, spec, probe, meas_hbm, right_hbm, left_hbm, kern_hbm, gbuf, *scratch):
    ext, full, meas, right, left, kern, canvas, pgrad, xa, xb, ya, yb, patch, wave = scratch[:14]
    selecting, bufs, sems = scratch[14:20], scratch[20:30], scratch[30:]
    loads = [
        pltpu.make_async_copy(src, dst, sems[0].at[k])
        for k, (src, dst) in enumerate([(meas_hbm, meas), (right_hbm, right), (left_hbm, left), (kern_hbm, kern)])
    ]
    for copy in loads:
        copy.start()
    at = Place(ns, nt)
    z = at.z
    greet(
        [(s, at.tile_at(d)) for s in (at.s, at.s_y) for d in range(1, nt)]
        + [(at.s_at_z(z + d), at.t) for d in (1, -1, 2, -2, 5, -5, 6, -6)] + [(at.s_y, at.t), (at.s_core, at.t)]
    )

    def split_own():
        split_rows(spec, selecting[0], 0, spec.shape[1], range(spec.shape[0]))

    share_later, finish, drain = gather_stage(at, nt, spec, probe, ext, full, sems[1:10], split_own)
    for copy in loads:
        copy.wait()
    window_stage(at.t, off, ext, full, meas, right, left, kern, canvas, pgrad, xa, xb, ya, yb, patch, wave, *selecting,
                 share_later, finish)
    sum_stage(at, nt, canvas, pgrad, gbuf, bufs, sems[10:], drain)


def place_kernel(ns, nt, gbuf, out, pout):
    z = Place(ns, nt).z
    nz = gbuf.shape[1]
    lanes = gbuf.shape[4]
    for j in range(nz):
        slot = lax.rem(j - z + OWN + nz, nz)
        for c in range(2):
            for k in range(2):
                for l in range(4):
                    out[2 * c + k, j, :, lanes * l:lanes * (l + 1)] = gbuf[c, slot, 4 * k + l]
            m, ri, r = j // 8, (j // 4) % 2, j % 4
            pout[2 * c + m, ri, pl.ds(4 * r, 4), :] = gbuf[c, slot, 8, 0:4]


def shards(ns, nt, specimen, probe_modes, offsets, intensity):
    slices, two, height, width = specimen.shape
    modes, _, prow, n = probe_modes.shape
    planes = slices * two
    nz = ns // 4
    sub = height // nz
    count = len(STREAMS)
    right, left, kernel = dft_tables(n)
    dma = pltpu.SemaphoreType.DMA
    vmem = pl.BlockSpec(memory_space=pltpu.VMEM)
    hbm = pl.BlockSpec(memory_space=pl.ANY)

    def f32(*shape):
        return pltpu.VMEM(shape, F32)

    def pair(*shape):
        return [dma(shape), dma(shape)]

    gathered = pl.pallas_call(
        partial(fused_kernel, ns, nt),
        name="gradient_sums",
        out_shape=jax.ShapeDtypeStruct((2, nz, 9, 8, n), F32),
        in_specs=[pl.BlockSpec(memory_space=pltpu.SMEM), vmem, vmem] + [hbm] * 4,
        out_specs=vmem,
        scratch_shapes=[
            f32(planes, 2 * height, width),
            f32(modes * two, n, n),
            f32(*intensity.shape),
            pltpu.VMEM(right.shape, BF16),
            pltpu.VMEM(left.shape, BF16),
            f32(2, n, n),
            f32(planes, 2, nz, sub, width),
            f32(modes, two, n, n),
            pltpu.VMEM((CAP * modes * n, 6 * n), BF16),
            pltpu.VMEM((CAP * modes * n, 6 * n), BF16),
            pltpu.VMEM((6 * n, CAP * modes * n), BF16),
            pltpu.VMEM((6 * n, CAP * modes * n), BF16),
            f32(CAP, planes, n, n),
            f32(CAP * modes, 2, n, n),
            pltpu.VMEM((2 * planes, 2 * height, width), BF16),
            pltpu.VMEM((width, CAP * n), BF16),
            pltpu.VMEM((CAP, 4 * height, planes * n), BF16),
            pltpu.VMEM((CAP, n, 2 * planes * n), BF16),
            pltpu.VMEM((planes * 2 * height, 2 * CAP * n), BF16),
            pltpu.VMEM((2 * CAP * n, width), BF16),
            f32(2, 2, nz, sub, width),
            f32(2, two, n, n),
            f32(nz, sub, width),
            f32(4, 5, sub, width),
            f32(4, 4, 5, sub, width),
            f32(5, sub, width),
            f32(nt // 2, 8, n),
            f32(2, sub, width),
            f32(2, 2, sub, width),
            f32(2, nt, 8, n),
        ]
        + [dma((4,))]
        + [dma((3,))] + pair(2) + pair(nt) + pair(2, 4) + pair(3)
        + pair(nz + 1) + pair(4, 4, count) + pair(3) + pair(2, nt) + pair(16) + pair(5),
        compiler_params=pltpu.CompilerParams(collective_id=0, has_side_effects=True, vmem_limit_bytes=VMEM_LIMIT),
    )(
        offsets, specimen.reshape(planes, height, width), probe_modes.reshape(modes * two, prow, n), intensity,
        jnp.asarray(right), jnp.asarray(left), jnp.asarray(kernel),
    )
    out, pout = pl.pallas_call(
        partial(place_kernel, ns, nt),
        name="place_rows",
        out_shape=(
            jax.ShapeDtypeStruct((planes, nz, sub, width), F32),
            jax.ShapeDtypeStruct((modes, two, prow, n), F32),
        ),
        in_specs=[vmem],
        out_specs=[vmem] * 2,
        compiler_params=pltpu.CompilerParams(vmem_limit_bytes=VMEM_LIMIT),
    )(gathered)
    return out.reshape(specimen.shape), pout


def solution(mesh):
    ns, nt = mesh.shape["scan"], mesh.shape["tile"]
    return jax.shard_map(
        partial(shards, ns, nt),
        mesh=mesh,
        in_specs=(
            P(None, None, "tile", None),
            P(None, None, "tile", None),
            P(None, "scan"),
            P("scan", None, None),
        ),
        out_specs=(P(None, None, "tile", None), P(None, None, "tile", None)),
        check_vma=False,
    )
```

```python
from functools import partial
import math

import jax
import jax.numpy as jnp
import numpy as np
from jax import lax
from jax.experimental import pallas as pl
from jax.experimental.pallas import tpu as pltpu
from jax.sharding import PartitionSpec as P

fresnel_phase = 40.0
F32 = jnp.float32
BF16 = jnp.bfloat16
MESH = pl.DeviceIdType.MESH
VMEM_LIMIT = 56 * 1024 * 1024
CAP = 2


def split_bf16(table):
    high = table.astype(BF16)
    low = (table - high.astype(np.float64)).astype(BF16)
    return np.asarray(high), np.asarray(low)


def dft_tables(n):
    k = np.arange(n)
    angle = (np.outer(k, k) % n) * (-2.0 * np.pi / n)
    re, im = np.cos(angle) / math.sqrt(n), np.sin(angle) / math.sqrt(n)
    forward = np.block([[re, im], [-im, re]])
    inverse = np.block([[re, -im], [im, re]])
    fh, fl = split_bf16(forward)
    ih, il = split_bf16(inverse)
    right = np.stack([np.concatenate([fh, fh, fl], 0), np.concatenate([ih, ih, il], 0)])
    left = np.stack([np.concatenate([ih, ih, il], 1), np.concatenate([fh, fh, fl], 1)])
    freq = np.fft.fftfreq(n)
    phi = -fresnel_phase * (freq[:, None] ** 2 + freq[None, :] ** 2)
    kernel = np.stack([np.cos(phi), np.sin(phi)]).astype(np.float32)
    return right, left, kernel


class Place:
    def __init__(self, ns, nt):
        self.ns, self.nt, self.nz = ns, nt, ns // 4
        s, t = lax.axis_index("scan"), lax.axis_index("tile")
        self.s, self.t = s, t
        self.core = lax.rem(s, 2)
        self.z = lax.rem(s // 2, self.nz)
        self.ylo = s // (2 * self.nz)
        self.s_core = s + 1 - 2 * self.core
        self.s_y = lax.rem(s + ns // 2, ns)

    def s_at_z(self, z):
        return (self.ylo * self.nz + lax.rem(z + self.nz, self.nz)) * 2 + self.core

    def tile_at(self, d):
        return lax.rem(self.t + d + self.nt, self.nt)


def remote(src, dst, send, recv, s, t):
    return pltpu.make_async_remote_copy(
        src_ref=src, dst_ref=dst, send_sem=send, recv_sem=recv,
        device_id={"scan": s, "tile": t}, device_id_type=MESH,
    )


def greet(peers):
    barrier = pltpu.get_barrier_semaphore()
    for s, t in peers:
        pl.semaphore_signal(barrier, inc=1, device_id={"scan": s, "tile": t}, device_id_type=MESH)
    pl.semaphore_wait(barrier, len(peers))


PARTS = 4


def gather_stage(at, nt, spec_ref, probe_ref, ext_ref, full_ref, sems, meanwhile):
    loc_sem, xs, xr, ps, pr, zs, zr, cs, cr = sems
    height = spec_ref.shape[1]
    prow, n = probe_ref.shape[1:]
    step = height // PARTS
    c, z = at.core, at.z
    part = lax.rem(z, PARTS)
    steps = [1, -1, 2, -2]
    groups = [c, 2 + c]
    first, last = at.t == 0, at.t == nt - 1

    def lower(g, lo, size):
        return ext_ref.at[groups[g], pl.ds(pl.multiple_of(height + part * step + lo, 8), size), :]

    def source(g):
        return spec_ref.at[groups[g], pl.ds(pl.multiple_of(part * step, 8), step), :]

    strips = [remote(source(g), lower(g, 0, step), xs.at[g], xr.at[g], at.s, at.tile_at(-1)) for g in range(2)]
    fillers = [pltpu.make_async_copy(source(g), lower(g, 0, step), loc_sem.at[1 + g]) for g in range(2)]
    four = pl.ds(4 * c, 4)
    mine = pl.ds(pl.multiple_of(at.t * prow, prow), prow)
    probes = [
        remote(probe_ref.at[four], full_ref.at[four, mine, :], ps.at[d], pr.at[d], at.s, at.tile_at(d))
        for d in range(1, nt)
    ]
    own_probe = pltpu.make_async_copy(probe_ref.at[four], full_ref.at[four, mine, :], loc_sem.at[0])

    def send(g):
        pl.when(jnp.logical_not(first))(strips[g].start)
        pl.when(last)(fillers[g].start)

    def arrived(g):
        pl.when(jnp.logical_not(last))(strips[g].wait_recv)
        pl.when(last)(fillers[g].wait)

    send(0)
    for copy in probes:
        copy.start()
    own_probe.start()
    send(1)
    meanwhile()

    cuts = [(0, step), (0, step), (0, step // 2), (step // 2, step // 2)]
    strip_z = [
        [
            remote(lower(g, *cuts[k]), lower(g, *cuts[k]), zs.at[g, k], zr.at[g, k], at.s_at_z(z + steps[k]), at.t)
            for k in range(4)
        ]
        for g in range(2)
    ]
    whole = [ext_ref.at[groups[g], pl.ds(height, height), :] for g in range(2)]
    whole += [full_ref.at[four]]
    shares = [remote(whole[k], whole[k], cs.at[k], cr.at[k], at.s_core, at.t) for k in range(3)]

    arrived(0)
    for copy in strip_z[0]:
        copy.start()
    arrived(1)
    for copy in strip_z[1]:
        copy.start()
    own_probe.wait()
    for copy in probes:
        copy.wait_recv()
    shares[2].start()
    for copy in strip_z[0]:
        copy.wait_recv()
    shares[0].start()
    shares[0].wait_recv()
    shares[2].wait_recv()

    def share_later():
        for copy in strip_z[1]:
            copy.wait_recv()
        shares[1].start()

    def finish():
        shares[1].wait_recv()

    def drain():
        for strip in strips:
            pl.when(jnp.logical_not(first))(strip.wait_send)
        for copy in probes + strip_z[0] + strip_z[1] + shares:
            copy.wait_send()

    return share_later, finish, drain


def put_right(ref, m, n, part, value):
    high = value.astype(BF16)
    low = (value - high.astype(F32)).astype(BF16)
    rows = pl.ds(m * n, n)
    ref[rows, pl.ds(part * n, n)] = high
    ref[rows, pl.ds((2 + part) * n, n)] = low
    ref[rows, pl.ds((4 + part) * n, n)] = high


def put_left(ref, m, n, part, value):
    high = value.astype(BF16)
    low = (value - high.astype(F32)).astype(BF16)
    cols = pl.ds(m * n, n)
    ref[pl.ds(part * n, n), cols] = high
    ref[pl.ds((2 + part) * n, n), cols] = low
    ref[pl.ds((4 + part) * n, n), cols] = high


def split_rows(source, parts, first, rows, planes):
    for p in planes:
        value = source[p]
        high = value.astype(BF16)
        parts[2 * p, pl.ds(first, rows)] = high
        parts[2 * p + 1, pl.ds(first, rows)] = (value - high.astype(F32)).astype(BF16)


def select(condition):
    return jnp.where(condition, 1.0, 0.0).astype(BF16)


def slots_of(off_ref, owner, height):
    per_group = off_ref.shape[1]
    far = 8 * height
    hits, corners = [], []
    for slot in range(CAP):
        rank = jnp.int32(0)
        row = jnp.int32(far)
        col = jnp.int32(0)
        chosen = []
        for b in range(per_group):
            here = ((off_ref[0, b] // height) == owner).astype(jnp.int32)
            hit = here * (rank == slot).astype(jnp.int32)
            row = row + hit * (off_ref[0, b] - owner * height - far)
            col = col + hit * off_ref[1, b]
            chosen.append(hit.astype(F32))
            rank = rank + here
        hits.append(chosen)
        corners.append((row, col))
    return hits, corners


def window_stage(at, slots, per_group, ext_ref, probe_ref, meas_ref, right_ref, left_ref, kern_ref,
                 canvas_ref, pgrad_ref, xa, xb, ya, yb, patch, wave, parts, cut, got, wgrad, got_w, tall, spread, put_got,
                 share_later, finish, swap_w, swap_p, swap_put):
    planes, height2, width = ext_ref.shape
    height = height2 // 2
    n = probe_ref.shape[1]
    modes = probe_ref.shape[0] // 2
    hits, corners = slots
    batch = [(slot, m) for slot in range(CAP) for m in range(modes)]

    def dot(a, b):
        return jnp.dot(a, b, preferred_element_type=F32)

    def mul_right(src, inverse):
        return dot(src[...], right_ref[inverse])

    def mul_left(src, inverse):
        return dot(left_ref[inverse], src[...])

    def right_parts(out, b):
        rows = out[b * n:(b + 1) * n]
        return rows[:, :n], rows[:, n:]

    def left_parts(out, b):
        cols = out[:, b * n:(b + 1) * n]
        return cols[:n], cols[n:]

    def right_to_left(src, dst, inverse):
        out = mul_right(src, inverse)
        for b in range(len(batch)):
            re, im = right_parts(out, b)
            put_left(dst, b, n, 0, re)
            put_left(dst, b, n, 1, im)

    def left_to_right(src, dst, inverse):
        out = mul_left(src, inverse)
        for b in range(len(batch)):
            re, im = left_parts(out, b)
            put_right(dst, b, n, 0, re)
            put_right(dst, b, n, 1, im)

    def through_kernel(src, dst, sign):
        out = mul_left(src, 0)
        kre, kim = kern_ref[0], kern_ref[1] * sign
        for b in range(len(batch)):
            re, im = left_parts(out, b)
            put_left(dst, b, n, 0, re * kre - im * kim)
            put_left(dst, b, n, 1, re * kim + im * kre)

    def iotas(*shape):
        return [lax.broadcasted_iota(jnp.int32, shape, axis) for axis in range(2)]

    i, j = iotas(width, n)
    for slot, (row, col) in enumerate(corners):
        cut[:, pl.ds(slot * n, n)] = select(i == j + col)

    def cut_windows(k):
        split_rows(ext_ref.at[:, pl.ds(height, height), :], parts, height, height, (2 * k, 2 * k + 1))
        out = dot(parts[pl.ds(4 * k, 4)].reshape(4 * height2, width), cut[...])
        for q in range(2):
            for part in range(2):
                rows = out[(2 * q + part) * height2:(2 * q + part + 1) * height2]
                for slot in range(CAP):
                    lanes = pl.ds((2 * k + q) * n, n)
                    got[slot, pl.ds(part * height2, height2), lanes] = rows[:, slot * n:(slot + 1) * n].astype(BF16)
        i, j = iotas(n, height2)
        for slot, (row, _) in enumerate(corners):
            pick = select(j == i + row)
            out = dot(jnp.concatenate([pick, pick], 1), got[slot, :, pl.ds(2 * k * n, 2 * n)])
            for q in range(2):
                patch[slot, 2 * k + q] = out[:, q * n:(q + 1) * n]

    cut_windows(0)
    for b, (slot, m) in enumerate(batch):
        pre, pim = probe_ref[2 * m], probe_ref[2 * m + 1]
        put_right(xa, b, n, 0, pre * patch[slot, 0] - pim * patch[slot, 1])
        put_right(xa, b, n, 1, pre * patch[slot, 1] + pim * patch[slot, 0])
    right_to_left(xa, ya, 0)
    through_kernel(ya, yb, 1.0)
    share_later()
    left_to_right(yb, xb, 1)
    finish()
    cut_windows(1)
    out = mul_right(xb, 1)
    for b, (slot, m) in enumerate(batch):
        re, im = right_parts(out, b)
        wave[b, 0] = re
        wave[b, 1] = im
        put_right(xa, b, n, 0, re * patch[slot, 2] - im * patch[slot, 3])
        put_right(xa, b, n, 1, re * patch[slot, 3] + im * patch[slot, 2])
    right_to_left(xa, ya, 0)
    out = mul_left(ya, 0)
    for slot in range(CAP):
        weight = sum(hits[slot])
        measured = hits[slot][0] * meas_ref[0]
        for b in range(1, per_group):
            measured = measured + hits[slot][b] * meas_ref[b]
        model = jnp.zeros((n, n), F32)
        for m in range(modes):
            re, im = left_parts(out, slot * modes + m)
            model = model + re * re + im * im
        twice = (2.0 * weight) * (model - measured)
        for m in range(modes):
            b = slot * modes + m
            re, im = left_parts(out, b)
            put_left(yb, b, n, 0, twice * re)
            put_left(yb, b, n, 1, twice * im)
    left_to_right(yb, xb, 1)
    out = mul_right(xb, 1)

    for slot in range(CAP):
        gre = jnp.zeros((n, n), F32)
        gim = jnp.zeros((n, n), F32)
        for m in range(modes):
            b = slot * modes + m
            re, im = right_parts(out, b)
            wre, wim = wave[b, 0], wave[b, 1]
            gre = gre + wre * re + wim * im
            gim = gim + wre * im - wim * re
            put_right(xa, b, n, 0, patch[slot, 2] * re + patch[slot, 3] * im)
            put_right(xa, b, n, 1, patch[slot, 2] * im - patch[slot, 3] * re)
        wgrad[slot, 2] = gre
        wgrad[slot, 3] = gim
    right_to_left(xa, ya, 0)
    through_kernel(ya, yb, -1.0)
    left_to_right(yb, xb, 1)
    out = mul_right(xb, 1)
    for m in range(modes):
        pgre = jnp.zeros((n, n), F32)
        pgim = jnp.zeros((n, n), F32)
        for slot in range(CAP):
            re, im = right_parts(out, slot * modes + m)
            pgre = pgre + patch[slot, 0] * re + patch[slot, 1] * im
            pgim = pgim + patch[slot, 0] * im - patch[slot, 1] * re
        pgrad_ref[m, 0] = pgre
        pgrad_ref[m, 1] = pgim
    swap_p.start()
    for slot in range(CAP):
        hre = jnp.zeros((n, n), F32)
        him = jnp.zeros((n, n), F32)
        for m in range(modes):
            re, im = right_parts(out, slot * modes + m)
            pre, pim = probe_ref[2 * m], probe_ref[2 * m + 1]
            hre = hre + pre * re + pim * im
            him = him + pre * im - pim * re
        wgrad[slot, 0] = hre
        wgrad[slot, 1] = him

    swap_w.start()
    i, j = iotas(height2, n)
    u, v = iotas(n, width)

    def put(e, row, col, windows):
        pieces = []
        for value in windows:
            high = value.astype(BF16)
            pieces += [high, (value - high.astype(F32)).astype(BF16)]
        out = dot(select(i == j + row), jnp.concatenate(pieces, 1))
        columns = select(v == u + col)
        for part in range(2):
            lanes = pl.ds((2 * e + part) * n, n)
            for q in range(2):
                piece = out[:, (2 * q + part) * n:(2 * q + part + 1) * n]
                tall[pl.ds(q * height2, height2), lanes] = piece.astype(BF16)
            spread[pl.ds((2 * e + part) * n, n), :] = columns

    for slot, (row, col) in enumerate(corners):
        put(slot, row, col, [wgrad[slot, 2 * at.core + q] for q in range(2)])
    swap_put.wait_recv()
    swap_w.wait_recv()
    for slot in range(CAP):
        row, col = put_got[2 * slot:2 * slot + 1, :n], put_got[2 * slot + 1:2 * slot + 2, :]
        put(CAP + slot, row, col, [got_w[slot, q] for q in range(2)])
    canvas_ref[...] = dot(tall[...], spread[...]).reshape(canvas_ref.shape)


STREAMS = ((0, 2), (2, 2), (4, 1))


OWN = 7


def sum_stage(at, nt, canvas, pgrad, gbuf, bufs, sems, swap_p, drain):
    got_p, pacc, chain, mine, pmine, ybuf, rimbuf, tbuf = bufs
    us, ur, ms, mr, ts, tr, gs, gr, ks, kr = sems
    nz = at.nz
    core, z = at.core, at.z
    lanes = 128

    def chunk(i):
        return lax.rem(i + 2 * nz, nz)

    def probe_rows():
        swap_p.wait_recv()
        for m in range(2):
            for ri in range(2):
                whole = pgrad[2 * core + m, ri] + got_p[m, ri]
                for r in range(4):
                    j = (2 * m + ri) * 4 + r
                    for t in range(nt):
                        piece = whole[16 * t + 4 * r:16 * t + 4 * r + 4]
                        pacc[j, 0, pl.ds(4 * (t % 2), 4), pl.ds(lanes * (t // 2), lanes)] = piece

    def local(k, idx):
        return pacc[chunk(z + k), 0] if idx == 4 else canvas[idx % 2, idx // 2, chunk(z + k)]

    def local_part(k, p):
        return pacc.at[chunk(z + k)] if p == 2 else canvas.at[:, p, chunk(z + k)]

    chains = [(8, 1, 4, True), (-7, -1, 3, True), (4, 1, 4, False), (-4, -1, 4, False)]
    count = len(STREAMS)

    def target(q, i):
        return chains[q][0] - i * chains[q][1]

    def hop(q, i, p):
        _, way, hops, jumps = chains[q]
        part = pl.ds(*STREAMS[p])
        src = local_part(target(q, 0), p) if i == 0 else chain.at[q, i - 1, part]
        to = target(q, i) if jumps and i == hops - 1 else way
        return remote(src, chain.at[q, i, part], us.at[q, i, p], ur.at[q, i, p], at.s_at_z(z + to), at.t)

    def span(p):
        return range(STREAMS[p][0], STREAMS[p][0] + STREAMS[p][1])

    for p in range(count - 1):
        for q in range(4):
            hop(q, 0, p).start()
    probe_rows()
    for q in range(4):
        hop(q, 0, count - 1).start()
    for i in range(4):
        for p in range(count):
            for q in range(4):
                if i < chains[q][2]:
                    hop(q, i, p).wait_recv()
                if i + 1 < chains[q][2]:
                    for idx in span(p):
                        chain[q, i, idx] += local(target(q, i + 1), idx)
                    hop(q, i + 1, p).start()
    for idx in range(5):
        total = local(0, idx)
        for q in range(4):
            total = total + chain[q, chains[q][2] - 1, idx]
        mine[idx] = total
    for q in range(nt // 2):
        pmine[q] = mine[4, :, lanes * q:lanes * (q + 1)]

    to_y = remote(mine.at[pl.ds(0, 2)], ybuf, ms.at[0], mr.at[0], at.s_y, at.t)
    rim_a = remote(mine.at[pl.ds(2, 2)], rimbuf.at[0], ms.at[1], mr.at[1], at.s, at.tile_at(1))
    rim_b = remote(mine.at[pl.ds(2, 2)], rimbuf.at[1], ms.at[2], mr.at[2], at.s_y, at.tile_at(1))
    tiles = [
        remote(pmine.at[at.tile_at(d) // 2], tbuf.at[at.ylo, at.t], ts.at[e, d], tr.at[e, d], s, at.tile_at(d))
        for e, s in ((0, at.s), (1, at.s_y)) for d in range(e ^ 1, nt)
    ]
    rim_b.start()
    rim_a.start()
    to_y.start()
    for copy in tiles:
        copy.start()
    tbuf[at.ylo, at.t] = pmine[at.t // 2]
    to_y.wait_recv()
    rim_a.wait_recv()
    rim_b.wait_recv()
    for k in range(2):
        final = (mine[k] + ybuf[k]) + (rimbuf[0, k] + rimbuf[1, k])
        for l in range(4):
            gbuf[core, OWN, 4 * k + l] = final[:, lanes * l:lanes * (l + 1)]
    for copy in tiles:
        copy.wait_recv()
    total = tbuf[0, 0]
    for k in range(1, 2 * nt):
        total = total + tbuf[k // nt, k % nt]
    gbuf[core, OWN, 8] = jnp.where(lax.rem(at.t, 2) == 1, pltpu.roll(total, 4, 0), total)

    def pass_on(i, k, to, part=slice(0, 9)):
        new = k - to + 16 * (k - to < -OWN)
        part = pl.ds(part.start, part.stop - part.start)
        return remote(gbuf.at[core, k + OWN, part], gbuf.at[core, new + OWN, part], gs.at[i], gr.at[i], at.s_at_z(z + to), at.t)

    def share(k, lo, hi):
        part = gbuf.at[core, pl.ds(lo + OWN, hi - lo + 1)]
        return remote(part, part, ks.at[k], kr.at[k], at.s_core, at.t)

    top, low = slice(0, 4), slice(4, 9)
    far = [pass_on(0, 0, 6), pass_on(1, 0, -6)]
    near = [pass_on(2, 0, 1), pass_on(3, 0, -1), pass_on(4, 0, 2), pass_on(5, 0, -2)]
    after_near = [pass_on(6, 2, -1), pass_on(7, 2, -2), pass_on(8, -2, 1), pass_on(9, -2, 2)]
    after_far = [
        pass_on(10, 6, -1), pass_on(11, 6, 1), pass_on(12, 6, -2, top),
        pass_on(13, -6, 1), pass_on(14, -6, -1), pass_on(15, -6, 2, low),
    ]
    shares = [share(0, -2, 2), share(1, 3, 4), share(2, -4, -3), share(3, 5, 8), share(4, -7, -5)]
    for copy in far + near:
        copy.start()
    drain()
    for copy in [to_y, rim_a, rim_b] + tiles:
        copy.wait_send()
    for q in range(4):
        for i in range(chains[q][2]):
            for p in range(count):
                hop(q, i, p).wait_send()
    near[3].wait_recv()
    near[2].wait_recv()
    near[1].wait_recv()
    near[0].wait_recv()
    for copy in after_near:
        copy.start()
    far[0].wait_recv()
    far[1].wait_recv()
    for copy in after_far:
        copy.start()
    shares[0].start()
    for copy in after_near:
        copy.wait_recv()
    shares[1].start()
    shares[2].start()
    for copy in after_far:
        copy.wait_recv()
    shares[3].start()
    shares[4].start()
    for copy in shares:
        copy.wait_recv()

    for copy in far + near + after_near + after_far + shares:
        copy.wait_send()


def fused_kernel(ns, nt, off, spec, probe, meas_hbm, right_hbm, left_hbm, kern_hbm, gbuf, *scratch):
    ext, full, meas, right, left, kern, canvas, pgrad, xa, xb, ya, yb, patch, wave = scratch[:14]
    selecting, put_own, bufs, sems = scratch[14:22], scratch[22], scratch[23:31], scratch[31:]
    loads = [
        pltpu.make_async_copy(src, dst, sems[0].at[k])
        for k, (src, dst) in enumerate([(meas_hbm, meas), (right_hbm, right), (left_hbm, left), (kern_hbm, kern)])
    ]
    for copy in loads:
        copy.start()
    at = Place(ns, nt)
    z = at.z
    greet(
        [(s, at.tile_at(d)) for s in (at.s, at.s_y) for d in range(1, nt)]
        + [(at.s_at_z(z + d), at.t) for d in (1, -1, 2, -2, 5, -5, 6, -6)] + [(at.s_y, at.t), (at.s_core, at.t)]
    )

    slots = slots_of(off, at.t, spec.shape[1])
    corners = sum(slots[1], ())
    lines = lax.broadcasted_iota(jnp.int32, put_own.shape, 0)
    places = jnp.zeros(put_own.shape, jnp.int32)
    for k, value in enumerate(corners):
        places = jnp.where(lines == k, value, places)
    put_own[...] = places
    wgrad, got_w, put_got = selecting[3], selecting[4], selecting[7]
    cs, cr = sems[10:12]
    swap_put = remote(put_own, put_got, cs.at[0], cr.at[0], at.s_core, at.t)
    swap_w = remote(wgrad.at[:, pl.ds(2 - 2 * at.core, 2)], got_w, cs.at[1], cr.at[1], at.s_core, at.t)
    swap_p = remote(pgrad.at[pl.ds(2 - 2 * at.core, 2)], bufs[0], cs.at[2], cr.at[2], at.s_core, at.t)

    def split_own():
        swap_put.start()
        split_rows(spec, selecting[0], 0, spec.shape[1], range(spec.shape[0]))

    share_later, finish, drain = gather_stage(at, nt, spec, probe, ext, full, sems[1:10], split_own)
    for copy in loads:
        copy.wait()
    window_stage(at, slots, off.shape[1], ext, full, meas, right, left, kern, canvas, pgrad, xa, xb, ya, yb, patch, wave, *selecting,
                 share_later, finish, swap_w, swap_p, swap_put)

    def drain_all():
        drain()
        for copy in (swap_put, swap_w, swap_p):
            copy.wait_send()

    sum_stage(at, nt, canvas, pgrad, gbuf, bufs, sems[12:], swap_p, drain_all)


def place_kernel(ns, nt, gbuf, out, pout):
    z = Place(ns, nt).z
    nz = gbuf.shape[1]
    lanes = gbuf.shape[4]
    for j in range(nz):
        slot = lax.rem(j - z + OWN + nz, nz)
        for c in range(2):
            for k in range(2):
                for l in range(4):
                    out[2 * c + k, j, :, lanes * l:lanes * (l + 1)] = gbuf[c, slot, 4 * k + l]
            m, ri, r = j // 8, (j // 4) % 2, j % 4
            pout[2 * c + m, ri, pl.ds(4 * r, 4), :] = gbuf[c, slot, 8, 0:4]


def shards(ns, nt, specimen, probe_modes, offsets, intensity):
    slices, two, height, width = specimen.shape
    modes, _, prow, n = probe_modes.shape
    planes = slices * two
    nz = ns // 4
    sub = height // nz
    count = len(STREAMS)
    right, left, kernel = dft_tables(n)
    dma = pltpu.SemaphoreType.DMA
    vmem = pl.BlockSpec(memory_space=pltpu.VMEM)
    hbm = pl.BlockSpec(memory_space=pl.ANY)

    def f32(*shape):
        return pltpu.VMEM(shape, F32)

    def pair(*shape):
        return [dma(shape), dma(shape)]

    gathered = pl.pallas_call(
        partial(fused_kernel, ns, nt),
        name="gradient_sums",
        out_shape=jax.ShapeDtypeStruct((2, nz, 9, 8, n), F32),
        in_specs=[pl.BlockSpec(memory_space=pltpu.SMEM), vmem, vmem] + [hbm] * 4,
        out_specs=vmem,
        scratch_shapes=[
            f32(planes, 2 * height, width),
            f32(modes * two, n, n),
            f32(*intensity.shape),
            pltpu.VMEM(right.shape, BF16),
            pltpu.VMEM(left.shape, BF16),
            f32(2, n, n),
            f32(2, 2, nz, sub, width),
            f32(modes, two, n, n),
            pltpu.VMEM((CAP * modes * n, 6 * n), BF16),
            pltpu.VMEM((CAP * modes * n, 6 * n), BF16),
            pltpu.VMEM((6 * n, CAP * modes * n), BF16),
            pltpu.VMEM((6 * n, CAP * modes * n), BF16),
            f32(CAP, planes, n, n),
            f32(CAP * modes, 2, n, n),
            pltpu.VMEM((2 * planes, 2 * height, width), BF16),
            pltpu.VMEM((width, CAP * n), BF16),
            pltpu.VMEM((CAP, 4 * height, planes * n), BF16),
            f32(CAP, planes, n, n),
            f32(CAP, 2, n, n),
            pltpu.VMEM((4 * height, 4 * CAP * n), BF16),
            pltpu.VMEM((4 * CAP * n, width), BF16),
            pltpu.VMEM((8, width), jnp.int32),
            pltpu.VMEM((8, width), jnp.int32),
            f32(2, two, n, n),
            f32(nz, 1, sub, width),
            f32(4, 4, 5, sub, width),
            f32(5, sub, width),
            f32(nt // 2, 8, n),
            f32(2, sub, width),
            f32(2, 2, sub, width),
            f32(2, nt, 8, n),
        ]
        + [dma((4,))]
        + [dma((3,))] + pair(2) + pair(nt) + pair(2, 4) + pair(3)
        + pair(3) + pair(4, 4, count) + pair(3) + pair(2, nt) + pair(16) + pair(5),
        compiler_params=pltpu.CompilerParams(collective_id=0, has_side_effects=True, vmem_limit_bytes=VMEM_LIMIT),
    )(
        offsets, specimen.reshape(planes, height, width), probe_modes.reshape(modes * two, prow, n), intensity,
        jnp.asarray(right), jnp.asarray(left), jnp.asarray(kernel),
    )
    out, pout = pl.pallas_call(
        partial(place_kernel, ns, nt),
        name="place_rows",
        out_shape=(
            jax.ShapeDtypeStruct((planes, nz, sub, width), F32),
            jax.ShapeDtypeStruct((modes, two, prow, n), F32),
        ),
        in_specs=[vmem],
        out_specs=[vmem] * 2,
        compiler_params=pltpu.CompilerParams(vmem_limit_bytes=VMEM_LIMIT),
    )(gathered)
    return out.reshape(specimen.shape), pout


def solution(mesh):
    ns, nt = mesh.shape["scan"], mesh.shape["tile"]
    return jax.shard_map(
        partial(shards, ns, nt),
        mesh=mesh,
        in_specs=(
            P(None, None, "tile", None),
            P(None, None, "tile", None),
            P(None, "scan"),
            P("scan", None, None),
        ),
        out_specs=(P(None, None, "tile", None), P(None, None, "tile", None)),
        check_vma=False,
    )
```

```python
from functools import partial
import math

import jax
import jax.numpy as jnp
import numpy as np
from jax import lax
from jax.experimental import pallas as pl
from jax.experimental.pallas import tpu as pltpu
from jax.sharding import PartitionSpec as P

fresnel_phase = 40.0
F32 = jnp.float32
BF16 = jnp.bfloat16
MESH = pl.DeviceIdType.MESH
VMEM_LIMIT = 56 * 1024 * 1024
CAP = 2


def split_bf16(table):
    high = table.astype(BF16)
    low = (table - high.astype(np.float64)).astype(BF16)
    return np.asarray(high), np.asarray(low)


def dft_tables(n):
    k = np.arange(n)
    angle = (np.outer(k, k) % n) * (-2.0 * np.pi / n)
    re, im = np.cos(angle) / math.sqrt(n), np.sin(angle) / math.sqrt(n)
    forward = np.block([[re, im], [-im, re]])
    inverse = np.block([[re, -im], [im, re]])
    fh, fl = split_bf16(forward)
    ih, il = split_bf16(inverse)
    right = np.stack([np.concatenate([fh, fh, fl], 0), np.concatenate([ih, ih, il], 0)])
    left = np.stack([np.concatenate([ih, ih, il], 1), np.concatenate([fh, fh, fl], 1)])
    freq = np.fft.fftfreq(n)
    phi = -fresnel_phase * (freq[:, None] ** 2 + freq[None, :] ** 2)
    kernel = np.stack([np.cos(phi), np.sin(phi)]).astype(np.float32)
    return right, left, kernel


class Place:
    def __init__(self, ns, nt):
        self.ns, self.nt, self.nz = ns, nt, ns // 4
        s, t = lax.axis_index("scan"), lax.axis_index("tile")
        self.s, self.t = s, t
        self.core = lax.rem(s, 2)
        self.z = lax.rem(s // 2, self.nz)
        self.ylo = s // (2 * self.nz)
        self.s_core = s + 1 - 2 * self.core
        self.s_y = lax.rem(s + ns // 2, ns)

    def s_at_z(self, z):
        return (self.ylo * self.nz + lax.rem(z + self.nz, self.nz)) * 2 + self.core

    def tile_at(self, d):
        return lax.rem(self.t + d + self.nt, self.nt)


def remote(src, dst, send, recv, s, t):
    return pltpu.make_async_remote_copy(
        src_ref=src, dst_ref=dst, send_sem=send, recv_sem=recv,
        device_id={"scan": s, "tile": t}, device_id_type=MESH,
    )


def greet(peers):
    barrier = pltpu.get_barrier_semaphore()
    for s, t in peers:
        pl.semaphore_signal(barrier, inc=1, device_id={"scan": s, "tile": t}, device_id_type=MESH)
    pl.semaphore_wait(barrier, len(peers))


PARTS = 4


def gather_stage(at, nt, spec_ref, probe_ref, ext_ref, full_ref, sems, meanwhile):
    loc_sem, xs, xr, ps, pr, zs, zr, cs, cr = sems
    height = spec_ref.shape[1]
    prow, n = probe_ref.shape[1:]
    step = height // PARTS
    c, z = at.core, at.z
    part = lax.rem(z, PARTS)
    steps = [1, -1, 2, -2]
    groups = [c, 2 + c]
    first, last = at.t == 0, at.t == nt - 1

    def lower(g, lo, size):
        return ext_ref.at[groups[g], pl.ds(pl.multiple_of(height + part * step + lo, 8), size), :]

    def source(g):
        return spec_ref.at[groups[g], pl.ds(pl.multiple_of(part * step, 8), step), :]

    strips = [remote(source(g), lower(g, 0, step), xs.at[g], xr.at[g], at.s, at.tile_at(-1)) for g in range(2)]
    fillers = [pltpu.make_async_copy(source(g), lower(g, 0, step), loc_sem.at[1 + g]) for g in range(2)]
    four = pl.ds(4 * c, 4)
    mine = pl.ds(pl.multiple_of(at.t * prow, prow), prow)
    probes = [
        remote(probe_ref.at[four], full_ref.at[four, mine, :], ps.at[d], pr.at[d], at.s, at.tile_at(d))
        for d in range(1, nt)
    ]
    own_probe = pltpu.make_async_copy(probe_ref.at[four], full_ref.at[four, mine, :], loc_sem.at[0])

    def send(g):
        pl.when(jnp.logical_not(first))(strips[g].start)
        pl.when(last)(fillers[g].start)

    def arrived(g):
        pl.when(jnp.logical_not(last))(strips[g].wait_recv)
        pl.when(last)(fillers[g].wait)

    send(0)
    for copy in probes:
        copy.start()
    own_probe.start()
    send(1)
    meanwhile()

    cuts = [(0, step), (0, step), (0, step // 2), (step // 2, step // 2)]
    strip_z = [
        [
            remote(lower(g, *cuts[k]), lower(g, *cuts[k]), zs.at[g, k], zr.at[g, k], at.s_at_z(z + steps[k]), at.t)
            for k in range(4)
        ]
        for g in range(2)
    ]
    whole = [ext_ref.at[groups[g], pl.ds(height, height), :] for g in range(2)]
    whole += [full_ref.at[four]]
    shares = [remote(whole[k], whole[k], cs.at[k], cr.at[k], at.s_core, at.t) for k in range(3)]

    arrived(0)
    for copy in strip_z[0]:
        copy.start()
    arrived(1)
    for copy in strip_z[1]:
        copy.start()
    own_probe.wait()
    for copy in probes:
        copy.wait_recv()
    shares[2].start()
    for copy in strip_z[0]:
        copy.wait_recv()
    shares[0].start()
    shares[0].wait_recv()
    shares[2].wait_recv()

    def share_later():
        for copy in strip_z[1]:
            copy.wait_recv()
        shares[1].start()

    def finish():
        shares[1].wait_recv()

    def drain():
        for strip in strips:
            pl.when(jnp.logical_not(first))(strip.wait_send)
        for copy in probes + strip_z[0] + strip_z[1] + shares:
            copy.wait_send()

    return share_later, finish, drain


def put_right(ref, m, n, part, value):
    high = value.astype(BF16)
    low = (value - high.astype(F32)).astype(BF16)
    rows = pl.ds(m * n, n)
    ref[rows, pl.ds(part * n, n)] = high
    ref[rows, pl.ds((2 + part) * n, n)] = low
    ref[rows, pl.ds((4 + part) * n, n)] = high


def put_left(ref, m, n, part, value):
    high = value.astype(BF16)
    low = (value - high.astype(F32)).astype(BF16)
    cols = pl.ds(m * n, n)
    ref[pl.ds(part * n, n), cols] = high
    ref[pl.ds((2 + part) * n, n), cols] = low
    ref[pl.ds((4 + part) * n, n), cols] = high


def split_rows(source, parts, first, rows, planes):
    for p in planes:
        value = source[p]
        high = value.astype(BF16)
        parts[2 * p, pl.ds(first, rows)] = high
        parts[2 * p + 1, pl.ds(first, rows)] = (value - high.astype(F32)).astype(BF16)


def select(condition):
    return jnp.where(condition, 1.0, 0.0).astype(BF16)


def slots_of(off_ref, owner, height):
    per_group = off_ref.shape[1]
    far = 8 * height
    hits, corners = [], []
    for slot in range(CAP):
        rank = jnp.int32(0)
        row = jnp.int32(far)
        col = jnp.int32(0)
        chosen = []
        for b in range(per_group):
            here = ((off_ref[0, b] // height) == owner).astype(jnp.int32)
            hit = here * (rank == slot).astype(jnp.int32)
            row = row + hit * (off_ref[0, b] - owner * height - far)
            col = col + hit * off_ref[1, b]
            chosen.append(hit.astype(F32))
            rank = rank + here
        hits.append(chosen)
        corners.append((row, col))
    return hits, corners


def window_stage(at, slots, per_group, ext_ref, probe_ref, meas_ref, right_ref, left_ref, kern_ref,
                 canvas_ref, pgrad_ref, xa, xb, ya, yb, patch, wave, parts, cut, got, wgrad, got_w, tall, spread, put_got,
                 share_later, finish, swap_w, swap_p, swap_put):
    planes, height2, width = ext_ref.shape
    height = height2 // 2
    n = probe_ref.shape[1]
    modes = probe_ref.shape[0] // 2
    hits, corners = slots
    batch = [(slot, m) for slot in range(CAP) for m in range(modes)]

    def dot(a, b):
        return jnp.dot(a, b, preferred_element_type=F32)

    def mul_right(src, inverse):
        return dot(src[...], right_ref[inverse])

    def mul_left(src, inverse):
        return dot(left_ref[inverse], src[...])

    def right_parts(out, b):
        rows = out[b * n:(b + 1) * n]
        return rows[:, :n], rows[:, n:]

    def left_parts(out, b):
        cols = out[:, b * n:(b + 1) * n]
        return cols[:n], cols[n:]

    def right_to_left(src, dst, inverse):
        out = mul_right(src, inverse)
        for b in range(len(batch)):
            re, im = right_parts(out, b)
            put_left(dst, b, n, 0, re)
            put_left(dst, b, n, 1, im)

    def left_to_right(src, dst, inverse):
        out = mul_left(src, inverse)
        for b in range(len(batch)):
            re, im = left_parts(out, b)
            put_right(dst, b, n, 0, re)
            put_right(dst, b, n, 1, im)

    def through_kernel(src, dst, sign):
        out = mul_left(src, 0)
        kre, kim = kern_ref[0], kern_ref[1] * sign
        for b in range(len(batch)):
            re, im = left_parts(out, b)
            put_left(dst, b, n, 0, re * kre - im * kim)
            put_left(dst, b, n, 1, re * kim + im * kre)

    def iotas(*shape):
        return [lax.broadcasted_iota(jnp.int32, shape, axis) for axis in range(2)]

    i, j = iotas(width, n)
    for slot, (row, col) in enumerate(corners):
        cut[:, pl.ds(slot * n, n)] = select(i == j + col)

    def cut_windows(k):
        split_rows(ext_ref.at[:, pl.ds(height, height), :], parts, height, height, (2 * k, 2 * k + 1))
        out = dot(parts[pl.ds(4 * k, 4)].reshape(4 * height2, width), cut[...])
        for q in range(2):
            for part in range(2):
                rows = out[(2 * q + part) * height2:(2 * q + part + 1) * height2]
                for slot in range(CAP):
                    lanes = pl.ds((2 * k + q) * n, n)
                    got[slot, pl.ds(part * height2, height2), lanes] = rows[:, slot * n:(slot + 1) * n].astype(BF16)
        i, j = iotas(n, height2)
        for slot, (row, _) in enumerate(corners):
            pick = select(j == i + row)
            out = dot(jnp.concatenate([pick, pick], 1), got[slot, :, pl.ds(2 * k * n, 2 * n)])
            for q in range(2):
                patch[slot, 2 * k + q] = out[:, q * n:(q + 1) * n]

    cut_windows(0)
    for b, (slot, m) in enumerate(batch):
        pre, pim = probe_ref[2 * m], probe_ref[2 * m + 1]
        put_right(xa, b, n, 0, pre * patch[slot, 0] - pim * patch[slot, 1])
        put_right(xa, b, n, 1, pre * patch[slot, 1] + pim * patch[slot, 0])
    right_to_left(xa, ya, 0)
    through_kernel(ya, yb, 1.0)
    share_later()
    left_to_right(yb, xb, 1)
    finish()
    cut_windows(1)
    out = mul_right(xb, 1)
    for b, (slot, m) in enumerate(batch):
        re, im = right_parts(out, b)
        wave[b, 0] = re
        wave[b, 1] = im
        put_right(xa, b, n, 0, re * patch[slot, 2] - im * patch[slot, 3])
        put_right(xa, b, n, 1, re * patch[slot, 3] + im * patch[slot, 2])
    right_to_left(xa, ya, 0)
    out = mul_left(ya, 0)
    for slot in range(CAP):
        weight = sum(hits[slot])
        measured = hits[slot][0] * meas_ref[0]
        for b in range(1, per_group):
            measured = measured + hits[slot][b] * meas_ref[b]
        model = jnp.zeros((n, n), F32)
        for m in range(modes):
            re, im = left_parts(out, slot * modes + m)
            model = model + re * re + im * im
        twice = (2.0 * weight) * (model - measured)
        for m in range(modes):
            b = slot * modes + m
            re, im = left_parts(out, b)
            put_left(yb, b, n, 0, twice * re)
            put_left(yb, b, n, 1, twice * im)
    left_to_right(yb, xb, 1)
    out = mul_right(xb, 1)

    for slot in range(CAP):
        gre = jnp.zeros((n, n), F32)
        gim = jnp.zeros((n, n), F32)
        for m in range(modes):
            b = slot * modes + m
            re, im = right_parts(out, b)
            wre, wim = wave[b, 0], wave[b, 1]
            gre = gre + wre * re + wim * im
            gim = gim + wre * im - wim * re
            put_right(xa, b, n, 0, patch[slot, 2] * re + patch[slot, 3] * im)
            put_right(xa, b, n, 1, patch[slot, 2] * im - patch[slot, 3] * re)
        wgrad[slot, 2] = gre
        wgrad[slot, 3] = gim
    right_to_left(xa, ya, 0)
    through_kernel(ya, yb, -1.0)
    left_to_right(yb, xb, 1)
    out = mul_right(xb, 1)
    for m in range(modes):
        pgre = jnp.zeros((n, n), F32)
        pgim = jnp.zeros((n, n), F32)
        for slot in range(CAP):
            re, im = right_parts(out, slot * modes + m)
            pgre = pgre + patch[slot, 0] * re + patch[slot, 1] * im
            pgim = pgim + patch[slot, 0] * im - patch[slot, 1] * re
        pgrad_ref[m, 0] = pgre
        pgrad_ref[m, 1] = pgim
    swap_p.start()
    for slot in range(CAP):
        hre = jnp.zeros((n, n), F32)
        him = jnp.zeros((n, n), F32)
        for m in range(modes):
            re, im = right_parts(out, slot * modes + m)
            pre, pim = probe_ref[2 * m], probe_ref[2 * m + 1]
            hre = hre + pre * re + pim * im
            him = him + pre * im - pim * re
        wgrad[slot, 0] = hre
        wgrad[slot, 1] = him

    swap_w.start()
    i, j = iotas(height2, n)
    u, v = iotas(n, width)

    def put(e, row, col, windows):
        pieces = []
        for value in windows:
            high = value.astype(BF16)
            pieces += [high, (value - high.astype(F32)).astype(BF16)]
        out = dot(select(i == j + row), jnp.concatenate(pieces, 1))
        columns = select(v == u + col)
        for part in range(2):
            lanes = pl.ds((2 * e + part) * n, n)
            for q in range(2):
                piece = out[:, (2 * q + part) * n:(2 * q + part + 1) * n]
                tall[pl.ds(q * height2, height2), lanes] = piece.astype(BF16)
            spread[pl.ds((2 * e + part) * n, n), :] = columns

    for slot, (row, col) in enumerate(corners):
        put(slot, row, col, [wgrad[slot, 2 * at.core + q] for q in range(2)])
    swap_put.wait_recv()
    swap_w.wait_recv()
    for slot in range(CAP):
        row, col = put_got[2 * slot:2 * slot + 1, :n], put_got[2 * slot + 1:2 * slot + 2, :]
        put(CAP + slot, row, col, [got_w[slot, q] for q in range(2)])
    canvas_ref[...] = dot(tall[...], spread[...]).reshape(canvas_ref.shape)


STREAMS = ((0, 2), (2, 2))


OWN = 7


def sum_stage(at, nt, canvas, pgrad, gbuf, bufs, sems, swap_p, drain):
    got_p, psum, tbuf, zsend, zbuf, pmine, pybuf, chain, mine, ybuf, rimbuf = bufs
    us, ur, ms, mr, ts, tr, zs, zr, gs, gr, ks, kr = sems
    nz = at.nz
    core, z = at.core, at.z
    lanes = 128

    def chunk(i):
        return lax.rem(i + 2 * nz, nz)

    pz = zsend.shape[0]
    prow = tbuf.shape[3]

    def rows_of(t):
        return pl.ds(pl.multiple_of(t * prow, prow), prow)

    tiles = [
        remote(psum.at[:, :, rows_of(at.tile_at(d)), :], tbuf.at[at.t], ts.at[d], tr.at[d], at.s, at.tile_at(d))
        for d in range(1, nt)
    ]
    zcopies = [
        remote(zsend.at[lax.rem(z + d, pz)], zbuf.at[z], zs.at[d], zr.at[d], at.s_at_z(z + d), at.t)
        for d in range(1, nz)
    ]
    py = remote(pmine, pybuf, ms.at[3], mr.at[3], at.s_y, at.t)

    def core_stage():
        swap_p.wait_recv()
        psum[...] = pgrad[pl.ds(2 * core, 2)] + got_p[...]
        for copy in tiles:
            copy.start()
        tbuf[at.t] = psum[:, :, rows_of(at.t), :]

    def tile_stage():
        for copy in tiles:
            copy.wait_recv()
        total = tbuf[0]
        for t in range(1, nt):
            total = total + tbuf[t]
        zsend[...] = total.reshape(zsend.shape)
        for copy in zcopies:
            copy.start()
        zbuf[z] = zsend[lax.rem(z, pz)]

    def z_stage():
        for copy in zcopies:
            copy.wait_recv()
        total = zbuf[0]
        for j in range(1, nz):
            total = total + zbuf[j]
        pmine[...] = total
        py.start()

    def local(k, idx):
        return canvas[idx % 2, idx // 2, chunk(z + k)]

    chains = [(8, 1, 4, True), (-7, -1, 3, True), (4, 1, 4, False), (-4, -1, 4, False)]
    count = len(STREAMS)

    def target(q, i):
        return chains[q][0] - i * chains[q][1]

    def hop(q, i, p):
        _, way, hops, jumps = chains[q]
        part = pl.ds(*STREAMS[p])
        src = canvas.at[:, p, chunk(z + target(q, 0))] if i == 0 else chain.at[q, i - 1, part]
        to = target(q, i) if jumps and i == hops - 1 else way
        return remote(src, chain.at[q, i, part], us.at[q, i, p], ur.at[q, i, p], at.s_at_z(z + to), at.t)

    def span(p):
        return range(STREAMS[p][0], STREAMS[p][0] + STREAMS[p][1])

    for p in range(count):
        for q in range(4):
            hop(q, 0, p).start()
    core_stage()
    for i in range(4):
        for p in range(count):
            for q in range(4):
                if i < chains[q][2]:
                    hop(q, i, p).wait_recv()
                if i + 1 < chains[q][2]:
                    for idx in span(p):
                        chain[q, i, idx] += local(target(q, i + 1), idx)
                    hop(q, i + 1, p).start()
        if i == 1:
            tile_stage()
        if i == 2:
            z_stage()
    for idx in range(4):
        total = local(0, idx)
        for q in range(4):
            total = total + chain[q, chains[q][2] - 1, idx]
        mine[idx] = total

    to_y = remote(mine.at[pl.ds(0, 2)], ybuf, ms.at[0], mr.at[0], at.s_y, at.t)
    rim_a = remote(mine.at[pl.ds(2, 2)], rimbuf.at[0], ms.at[1], mr.at[1], at.s, at.tile_at(1))
    rim_b = remote(mine.at[pl.ds(2, 2)], rimbuf.at[1], ms.at[2], mr.at[2], at.s_y, at.tile_at(1))
    rim_b.start()
    rim_a.start()
    to_y.start()
    py.wait_recv()
    gbuf[core, OWN, 8] = pmine[...] + pybuf[...]
    to_y.wait_recv()
    rim_a.wait_recv()
    rim_b.wait_recv()
    for k in range(2):
        final = (mine[k] + ybuf[k]) + (rimbuf[0, k] + rimbuf[1, k])
        for l in range(4):
            gbuf[core, OWN, 4 * k + l] = final[:, lanes * l:lanes * (l + 1)]

    def pass_on(i, k, to, part=slice(0, 9)):
        new = k - to + 16 * (k - to < -OWN)
        part = pl.ds(part.start, part.stop - part.start)
        return remote(gbuf.at[core, k + OWN, part], gbuf.at[core, new + OWN, part], gs.at[i], gr.at[i], at.s_at_z(z + to), at.t)

    def share(k, lo, hi):
        part = gbuf.at[core, pl.ds(lo + OWN, hi - lo + 1)]
        return remote(part, part, ks.at[k], kr.at[k], at.s_core, at.t)

    top, low = slice(0, 4), slice(4, 9)
    far = [pass_on(0, 0, 6), pass_on(1, 0, -6)]
    near = [pass_on(2, 0, 1), pass_on(3, 0, -1), pass_on(4, 0, 2), pass_on(5, 0, -2)]
    after_near = [pass_on(6, 2, -1), pass_on(7, 2, -2), pass_on(8, -2, 1), pass_on(9, -2, 2)]
    after_far = [
        pass_on(10, 6, -1), pass_on(11, 6, 1), pass_on(12, 6, -2, top),
        pass_on(13, -6, 1), pass_on(14, -6, -1), pass_on(15, -6, 2, low),
    ]
    shares = [share(0, -2, 2), share(1, 3, 4), share(2, -4, -3), share(3, 5, 8), share(4, -7, -5)]
    for copy in far + near:
        copy.start()
    drain()
    for copy in [to_y, rim_a, rim_b, py] + tiles + zcopies:
        copy.wait_send()
    for q in range(4):
        for i in range(chains[q][2]):
            for p in range(count):
                hop(q, i, p).wait_send()
    near[3].wait_recv()
    near[2].wait_recv()
    near[1].wait_recv()
    near[0].wait_recv()
    for copy in after_near:
        copy.start()
    far[0].wait_recv()
    far[1].wait_recv()
    for copy in after_far:
        copy.start()
    shares[0].start()
    for copy in after_near:
        copy.wait_recv()
    shares[1].start()
    shares[2].start()
    for copy in after_far:
        copy.wait_recv()
    shares[3].start()
    shares[4].start()
    for copy in shares:
        copy.wait_recv()

    for copy in far + near + after_near + after_far + shares:
        copy.wait_send()


def fused_kernel(ns, nt, off, spec, probe, meas_hbm, right_hbm, left_hbm, kern_hbm, gbuf, *scratch):
    ext, full, meas, right, left, kern, canvas, pgrad, xa, xb, ya, yb, patch, wave = scratch[:14]
    selecting, put_own, bufs, sems = scratch[14:22], scratch[22], scratch[23:34], scratch[34:]
    loads = [
        pltpu.make_async_copy(src, dst, sems[0].at[k])
        for k, (src, dst) in enumerate([(meas_hbm, meas), (right_hbm, right), (left_hbm, left), (kern_hbm, kern)])
    ]
    for copy in loads:
        copy.start()
    at = Place(ns, nt)
    z = at.z
    greet(
        [(s, at.tile_at(d)) for s in (at.s, at.s_y) for d in range(1, nt)]
        + [(at.s_at_z(z + d), at.t) for d in range(1, at.nz)] + [(at.s_y, at.t), (at.s_core, at.t)]
    )

    slots = slots_of(off, at.t, spec.shape[1])
    corners = sum(slots[1], ())
    lines = lax.broadcasted_iota(jnp.int32, put_own.shape, 0)
    places = jnp.zeros(put_own.shape, jnp.int32)
    for k, value in enumerate(corners):
        places = jnp.where(lines == k, value, places)
    put_own[...] = places
    wgrad, got_w, put_got = selecting[3], selecting[4], selecting[7]
    cs, cr = sems[10:12]
    swap_put = remote(put_own, put_got, cs.at[0], cr.at[0], at.s_core, at.t)
    swap_w = remote(wgrad.at[:, pl.ds(2 - 2 * at.core, 2)], got_w, cs.at[1], cr.at[1], at.s_core, at.t)
    swap_p = remote(pgrad.at[pl.ds(2 - 2 * at.core, 2)], bufs[0], cs.at[2], cr.at[2], at.s_core, at.t)

    def split_own():
        swap_put.start()
        split_rows(spec, selecting[0], 0, spec.shape[1], range(spec.shape[0]))

    share_later, finish, drain = gather_stage(at, nt, spec, probe, ext, full, sems[1:10], split_own)
    for copy in loads:
        copy.wait()
    window_stage(at, slots, off.shape[1], ext, full, meas, right, left, kern, canvas, pgrad, xa, xb, ya, yb, patch, wave, *selecting,
                 share_later, finish, swap_w, swap_p, swap_put)

    def drain_all():
        drain()
        for copy in (swap_put, swap_w, swap_p):
            copy.wait_send()

    sum_stage(at, nt, canvas, pgrad, gbuf, bufs, sems[12:], swap_p, drain_all)


def place_kernel(ns, nt, gbuf, out, pout):
    z = Place(ns, nt).z
    nz = gbuf.shape[1]
    lanes = gbuf.shape[4]
    for j in range(nz):
        slot = lax.rem(j - z + OWN + nz, nz)
        for c in range(2):
            for k in range(2):
                for l in range(4):
                    out[2 * c + k, j, :, lanes * l:lanes * (l + 1)] = gbuf[c, slot, 4 * k + l]
            if j < nz // 2:
                m, ri, h = j // 4, (j // 2) % 2, j % 2
                pout[2 * c + m, ri, pl.ds(8 * h, 8), :] = gbuf[c, slot, 8]


def shards(ns, nt, specimen, probe_modes, offsets, intensity):
    slices, two, height, width = specimen.shape
    modes, _, prow, n = probe_modes.shape
    planes = slices * two
    nz = ns // 4
    sub = height // nz
    count = len(STREAMS)
    right, left, kernel = dft_tables(n)
    dma = pltpu.SemaphoreType.DMA
    vmem = pl.BlockSpec(memory_space=pltpu.VMEM)
    hbm = pl.BlockSpec(memory_space=pl.ANY)

    def f32(*shape):
        return pltpu.VMEM(shape, F32)

    def pair(*shape):
        return [dma(shape), dma(shape)]

    gathered = pl.pallas_call(
        partial(fused_kernel, ns, nt),
        name="gradient_sums",
        out_shape=jax.ShapeDtypeStruct((2, nz, 9, 8, n), F32),
        in_specs=[pl.BlockSpec(memory_space=pltpu.SMEM), vmem, vmem] + [hbm] * 4,
        out_specs=vmem,
        scratch_shapes=[
            f32(planes, 2 * height, width),
            f32(modes * two, n, n),
            f32(*intensity.shape),
            pltpu.VMEM(right.shape, BF16),
            pltpu.VMEM(left.shape, BF16),
            f32(2, n, n),
            f32(2, 2, nz, sub, width),
            f32(modes, two, n, n),
            pltpu.VMEM((CAP * modes * n, 6 * n), BF16),
            pltpu.VMEM((CAP * modes * n, 6 * n), BF16),
            pltpu.VMEM((6 * n, CAP * modes * n), BF16),
            pltpu.VMEM((6 * n, CAP * modes * n), BF16),
            f32(CAP, planes, n, n),
            f32(CAP * modes, 2, n, n),
            pltpu.VMEM((2 * planes, 2 * height, width), BF16),
            pltpu.VMEM((width, CAP * n), BF16),
            pltpu.VMEM((CAP, 4 * height, planes * n), BF16),
            f32(CAP, planes, n, n),
            f32(CAP, 2, n, n),
            pltpu.VMEM((4 * height, 4 * CAP * n), BF16),
            pltpu.VMEM((4 * CAP * n, width), BF16),
            pltpu.VMEM((8, width), jnp.int32),
            pltpu.VMEM((8, width), jnp.int32),
            f32(2, two, n, n),
            f32(2, two, n, n),
            f32(nt, 2, two, prow, n),
            f32(2 * two * prow // 8, 8, n),
            f32(nz, 8, n),
            f32(8, n),
            f32(8, n),
            f32(4, 4, 4, sub, width),
            f32(4, sub, width),
            f32(2, sub, width),
            f32(2, 2, sub, width),
        ]
        + [dma((4,))]
        + [dma((3,))] + pair(2) + pair(nt) + pair(2, 4) + pair(3)
        + pair(3) + pair(4, 4, count) + pair(4) + pair(nt) + pair(nz) + pair(16) + pair(5),
        compiler_params=pltpu.CompilerParams(collective_id=0, has_side_effects=True, vmem_limit_bytes=VMEM_LIMIT),
    )(
        offsets, specimen.reshape(planes, height, width), probe_modes.reshape(modes * two, prow, n), intensity,
        jnp.asarray(right), jnp.asarray(left), jnp.asarray(kernel),
    )
    out, pout = pl.pallas_call(
        partial(place_kernel, ns, nt),
        name="place_rows",
        out_shape=(
            jax.ShapeDtypeStruct((planes, nz, sub, width), F32),
            jax.ShapeDtypeStruct((modes, two, prow, n), F32),
        ),
        in_specs=[vmem],
        out_specs=[vmem] * 2,
        compiler_params=pltpu.CompilerParams(vmem_limit_bytes=VMEM_LIMIT),
    )(gathered)
    return out.reshape(specimen.shape), pout


def solution(mesh):
    ns, nt = mesh.shape["scan"], mesh.shape["tile"]
    return jax.shard_map(
        partial(shards, ns, nt),
        mesh=mesh,
        in_specs=(
            P(None, None, "tile", None),
            P(None, None, "tile", None),
            P(None, "scan"),
            P("scan", None, None),
        ),
        out_specs=(P(None, None, "tile", None), P(None, None, "tile", None)),
        check_vma=False,
    )
```

```python
from functools import partial
import math

import jax
import jax.numpy as jnp
import numpy as np
from jax import lax
from jax.experimental import pallas as pl
from jax.experimental.pallas import tpu as pltpu
from jax.sharding import PartitionSpec as P

fresnel_phase = 40.0
F32 = jnp.float32
BF16 = jnp.bfloat16
MESH = pl.DeviceIdType.MESH
VMEM_LIMIT = 56 * 1024 * 1024
CAP = 2


def split_bf16(table):
    high = table.astype(BF16)
    low = (table - high.astype(np.float64)).astype(BF16)
    return np.asarray(high), np.asarray(low)


def dft_tables(n):
    k = np.arange(n)
    angle = (np.outer(k, k) % n) * (-2.0 * np.pi / n)
    re, im = np.cos(angle) / math.sqrt(n), np.sin(angle) / math.sqrt(n)
    forward = np.block([[re, im], [-im, re]])
    inverse = np.block([[re, -im], [im, re]])
    fh, fl = split_bf16(forward)
    ih, il = split_bf16(inverse)
    right = np.stack([np.concatenate([fh, fh, fl], 0), np.concatenate([ih, ih, il], 0)])
    left = np.stack([np.concatenate([ih, ih, il], 1), np.concatenate([fh, fh, fl], 1)])
    freq = np.fft.fftfreq(n)
    phi = -fresnel_phase * (freq[:, None] ** 2 + freq[None, :] ** 2)
    kernel = np.stack([np.cos(phi), np.sin(phi)]).astype(np.float32)
    return right, left, kernel


class Place:
    def __init__(self, ns, nt):
        self.ns, self.nt, self.nz = ns, nt, ns // 4
        s, t = lax.axis_index("scan"), lax.axis_index("tile")
        self.s, self.t = s, t
        self.core = lax.rem(s, 2)
        self.z = lax.rem(s // 2, self.nz)
        self.ylo = s // (2 * self.nz)
        self.s_core = s + 1 - 2 * self.core
        self.s_y = lax.rem(s + ns // 2, ns)

    def s_at_z(self, z):
        return (self.ylo * self.nz + lax.rem(z + self.nz, self.nz)) * 2 + self.core

    def tile_at(self, d):
        return lax.rem(self.t + d + self.nt, self.nt)


def remote(src, dst, send, recv, s, t):
    return pltpu.make_async_remote_copy(
        src_ref=src, dst_ref=dst, send_sem=send, recv_sem=recv,
        device_id={"scan": s, "tile": t}, device_id_type=MESH,
    )


def greet(peers):
    barrier = pltpu.get_barrier_semaphore()
    for s, t in peers:
        pl.semaphore_signal(barrier, inc=1, device_id={"scan": s, "tile": t}, device_id_type=MESH)
    pl.semaphore_wait(barrier, len(peers))


PARTS = 4


def gather_stage(at, nt, spec_ref, probe_ref, ext_ref, full_ref, sems, meanwhile):
    loc_sem, xs, xr, ps, pr, zs, zr, cs, cr = sems
    height = spec_ref.shape[1]
    prow, n = probe_ref.shape[1:]
    step = height // PARTS
    c, z = at.core, at.z
    part = lax.rem(z, PARTS)
    steps = [1, -1, 2, -2]
    groups = [c, 2 + c]
    first, last = at.t == 0, at.t == nt - 1

    def lower(g, lo, size):
        return ext_ref.at[groups[g], pl.ds(pl.multiple_of(height + part * step + lo, 8), size), :]

    def source(g):
        return spec_ref.at[groups[g], pl.ds(pl.multiple_of(part * step, 8), step), :]

    strips = [remote(source(g), lower(g, 0, step), xs.at[g], xr.at[g], at.s, at.tile_at(-1)) for g in range(2)]
    fillers = [pltpu.make_async_copy(source(g), lower(g, 0, step), loc_sem.at[1 + g]) for g in range(2)]
    four = pl.ds(4 * c, 4)
    mine = pl.ds(pl.multiple_of(at.t * prow, prow), prow)
    probes = [
        remote(probe_ref.at[four], full_ref.at[four, mine, :], ps.at[d], pr.at[d], at.s, at.tile_at(d))
        for d in range(1, nt)
    ]
    own_probe = pltpu.make_async_copy(probe_ref.at[four], full_ref.at[four, mine, :], loc_sem.at[0])

    def send(g):
        pl.when(jnp.logical_not(first))(strips[g].start)
        pl.when(last)(fillers[g].start)

    def arrived(g):
        pl.when(jnp.logical_not(last))(strips[g].wait_recv)
        pl.when(last)(fillers[g].wait)

    send(0)
    for copy in probes:
        copy.start()
    own_probe.start()
    send(1)
    meanwhile()

    cuts = [(0, step), (0, step), (0, step // 2), (step // 2, step // 2)]
    strip_z = [
        [
            remote(lower(g, *cuts[k]), lower(g, *cuts[k]), zs.at[g, k], zr.at[g, k], at.s_at_z(z + steps[k]), at.t)
            for k in range(4)
        ]
        for g in range(2)
    ]
    whole = [ext_ref.at[groups[g], pl.ds(height, height), :] for g in range(2)]
    whole += [full_ref.at[four]]
    shares = [remote(whole[k], whole[k], cs.at[k], cr.at[k], at.s_core, at.t) for k in range(3)]

    arrived(0)
    for copy in strip_z[0]:
        copy.start()
    arrived(1)
    for copy in strip_z[1]:
        copy.start()
    own_probe.wait()
    for copy in probes:
        copy.wait_recv()
    shares[2].start()
    for copy in strip_z[0]:
        copy.wait_recv()
    shares[0].start()
    shares[0].wait_recv()
    shares[2].wait_recv()

    def share_later():
        for copy in strip_z[1]:
            copy.wait_recv()
        shares[1].start()

    def finish():
        shares[1].wait_recv()

    def drain():
        for strip in strips:
            pl.when(jnp.logical_not(first))(strip.wait_send)
        for copy in probes + strip_z[0] + strip_z[1] + shares:
            copy.wait_send()

    return share_later, finish, drain


def put_right(ref, m, n, part, value):
    high = value.astype(BF16)
    low = (value - high.astype(F32)).astype(BF16)
    rows = pl.ds(m * n, n)
    ref[rows, pl.ds(part * n, n)] = high
    ref[rows, pl.ds((2 + part) * n, n)] = low
    ref[rows, pl.ds((4 + part) * n, n)] = high


def put_left(ref, m, n, part, value):
    high = value.astype(BF16)
    low = (value - high.astype(F32)).astype(BF16)
    cols = pl.ds(m * n, n)
    ref[pl.ds(part * n, n), cols] = high
    ref[pl.ds((2 + part) * n, n), cols] = low
    ref[pl.ds((4 + part) * n, n), cols] = high


def split_rows(source, parts, first, rows, planes):
    for p in planes:
        value = source[p]
        high = value.astype(BF16)
        parts[2 * p, pl.ds(first, rows)] = high
        parts[2 * p + 1, pl.ds(first, rows)] = (value - high.astype(F32)).astype(BF16)


def select(condition):
    return jnp.where(condition, 1.0, 0.0).astype(BF16)


def slots_of(off_ref, owner, height):
    per_group = off_ref.shape[1]
    far = 8 * height
    hits, corners = [], []
    for slot in range(CAP):
        rank = jnp.int32(0)
        row = jnp.int32(far)
        col = jnp.int32(0)
        chosen = []
        for b in range(per_group):
            here = ((off_ref[0, b] // height) == owner).astype(jnp.int32)
            hit = here * (rank == slot).astype(jnp.int32)
            row = row + hit * (off_ref[0, b] - owner * height - far)
            col = col + hit * off_ref[1, b]
            chosen.append(hit.astype(F32))
            rank = rank + here
        hits.append(chosen)
        corners.append((row, col))
    return hits, corners


def window_stage(at, slots, per_group, ext_ref, probe_ref, meas_ref, right_ref, left_ref, kern_ref,
                 canvas_ref, pgrad_ref, xa, xb, ya, yb, patch, wave, parts, cut, got, wgrad, got_w, tall, spread, put_got,
                 share_later, finish, swap_w, swap_p, swap_put):
    planes, height2, width = ext_ref.shape
    height = height2 // 2
    n = probe_ref.shape[1]
    modes = probe_ref.shape[0] // 2
    hits, corners = slots
    batch = [(slot, m) for slot in range(CAP) for m in range(modes)]

    def dot(a, b):
        return jnp.dot(a, b, preferred_element_type=F32)

    def mul_right(src, inverse):
        return dot(src[...], right_ref[inverse])

    def mul_left(src, inverse):
        return dot(left_ref[inverse], src[...])

    def right_parts(out, b):
        rows = out[b * n:(b + 1) * n]
        return rows[:, :n], rows[:, n:]

    def left_parts(out, b):
        cols = out[:, b * n:(b + 1) * n]
        return cols[:n], cols[n:]

    def right_to_left(src, dst, inverse):
        out = mul_right(src, inverse)
        for b in range(len(batch)):
            re, im = right_parts(out, b)
            put_left(dst, b, n, 0, re)
            put_left(dst, b, n, 1, im)

    def left_to_right(src, dst, inverse):
        out = mul_left(src, inverse)
        for b in range(len(batch)):
            re, im = left_parts(out, b)
            put_right(dst, b, n, 0, re)
            put_right(dst, b, n, 1, im)

    def through_kernel(src, dst, sign):
        out = mul_left(src, 0)
        kre, kim = kern_ref[0], kern_ref[1] * sign
        for b in range(len(batch)):
            re, im = left_parts(out, b)
            put_left(dst, b, n, 0, re * kre - im * kim)
            put_left(dst, b, n, 1, re * kim + im * kre)

    def iotas(*shape):
        return [lax.broadcasted_iota(jnp.int32, shape, axis) for axis in range(2)]

    i, j = iotas(width, n)
    for slot, (row, col) in enumerate(corners):
        cut[:, pl.ds(slot * n, n)] = select(i == j + col)

    def cut_windows(k):
        split_rows(ext_ref.at[:, pl.ds(height, height), :], parts, height, height, (2 * k, 2 * k + 1))
        out = dot(parts[pl.ds(4 * k, 4)].reshape(4 * height2, width), cut[...])
        for q in range(2):
            for part in range(2):
                rows = out[(2 * q + part) * height2:(2 * q + part + 1) * height2]
                for slot in range(CAP):
                    lanes = pl.ds((2 * k + q) * n, n)
                    got[slot, pl.ds(part * height2, height2), lanes] = rows[:, slot * n:(slot + 1) * n].astype(BF16)
        i, j = iotas(n, height2)
        for slot, (row, _) in enumerate(corners):
            pick = select(j == i + row)
            out = dot(jnp.concatenate([pick, pick], 1), got[slot, :, pl.ds(2 * k * n, 2 * n)])
            for q in range(2):
                patch[slot, 2 * k + q] = out[:, q * n:(q + 1) * n]

    cut_windows(0)
    for b, (slot, m) in enumerate(batch):
        pre, pim = probe_ref[2 * m], probe_ref[2 * m + 1]
        put_right(xa, b, n, 0, pre * patch[slot, 0] - pim * patch[slot, 1])
        put_right(xa, b, n, 1, pre * patch[slot, 1] + pim * patch[slot, 0])
    right_to_left(xa, ya, 0)
    through_kernel(ya, yb, 1.0)
    share_later()
    left_to_right(yb, xb, 1)
    finish()
    cut_windows(1)
    out = mul_right(xb, 1)
    for b, (slot, m) in enumerate(batch):
        re, im = right_parts(out, b)
        wave[b, 0] = re
        wave[b, 1] = im
        put_right(xa, b, n, 0, re * patch[slot, 2] - im * patch[slot, 3])
        put_right(xa, b, n, 1, re * patch[slot, 3] + im * patch[slot, 2])
    right_to_left(xa, ya, 0)
    out = mul_left(ya, 0)
    for slot in range(CAP):
        weight = sum(hits[slot])
        measured = hits[slot][0] * meas_ref[0]
        for b in range(1, per_group):
            measured = measured + hits[slot][b] * meas_ref[b]
        model = jnp.zeros((n, n), F32)
        for m in range(modes):
            re, im = left_parts(out, slot * modes + m)
            model = model + re * re + im * im
        twice = (2.0 * weight) * (model - measured)
        for m in range(modes):
            b = slot * modes + m
            re, im = left_parts(out, b)
            put_left(yb, b, n, 0, twice * re)
            put_left(yb, b, n, 1, twice * im)
    left_to_right(yb, xb, 1)
    out = mul_right(xb, 1)

    for slot in range(CAP):
        gre = jnp.zeros((n, n), F32)
        gim = jnp.zeros((n, n), F32)
        for m in range(modes):
            b = slot * modes + m
            re, im = right_parts(out, b)
            wre, wim = wave[b, 0], wave[b, 1]
            gre = gre + wre * re + wim * im
            gim = gim + wre * im - wim * re
            put_right(xa, b, n, 0, patch[slot, 2] * re + patch[slot, 3] * im)
            put_right(xa, b, n, 1, patch[slot, 2] * im - patch[slot, 3] * re)
        wgrad[slot, 2] = gre
        wgrad[slot, 3] = gim
    right_to_left(xa, ya, 0)
    through_kernel(ya, yb, -1.0)
    left_to_right(yb, xb, 1)
    out = mul_right(xb, 1)
    for m in range(modes):
        pgre = jnp.zeros((n, n), F32)
        pgim = jnp.zeros((n, n), F32)
        for slot in range(CAP):
            re, im = right_parts(out, slot * modes + m)
            pgre = pgre + patch[slot, 0] * re + patch[slot, 1] * im
            pgim = pgim + patch[slot, 0] * im - patch[slot, 1] * re
        pgrad_ref[m, 0] = pgre
        pgrad_ref[m, 1] = pgim
    swap_p.start()
    for slot in range(CAP):
        hre = jnp.zeros((n, n), F32)
        him = jnp.zeros((n, n), F32)
        for m in range(modes):
            re, im = right_parts(out, slot * modes + m)
            pre, pim = probe_ref[2 * m], probe_ref[2 * m + 1]
            hre = hre + pre * re + pim * im
            him = him + pre * im - pim * re
        wgrad[slot, 0] = hre
        wgrad[slot, 1] = him

    swap_w.start()
    i, j = iotas(height2, n)
    u, v = iotas(n, width)

    def put(e, row, col, windows):
        pieces = []
        for value in windows:
            high = value.astype(BF16)
            pieces += [high, (value - high.astype(F32)).astype(BF16)]
        out = dot(select(i == j + row), jnp.concatenate(pieces, 1))
        columns = select(v == u + col)
        for part in range(2):
            lanes = pl.ds((2 * e + part) * n, n)
            for q in range(2):
                piece = out[:, (2 * q + part) * n:(2 * q + part + 1) * n]
                tall[pl.ds(q * height2, height2), lanes] = piece.astype(BF16)
            spread[pl.ds((2 * e + part) * n, n), :] = columns

    for slot, (row, col) in enumerate(corners):
        put(slot, row, col, [wgrad[slot, 2 * at.core + q] for q in range(2)])
    swap_put.wait_recv()
    swap_w.wait_recv()
    for slot in range(CAP):
        row, col = put_got[2 * slot:2 * slot + 1, :n], put_got[2 * slot + 1:2 * slot + 2, :]
        put(CAP + slot, row, col, [got_w[slot, q] for q in range(2)])
    canvas_ref[...] = dot(tall[...], spread[...]).reshape(canvas_ref.shape)


STREAMS = ((0, 2), (2, 2))


OWN = 7


def sum_stage(at, nt, canvas, pgrad, gbuf, bufs, sems, swap_p, drain):
    got_p, psum, tbuf, zsend, zbuf, pmine, pybuf, chain, mine, ybuf, rimbuf = bufs
    us, ur, ms, mr, ts, tr, zs, zr, gs, gr, ks, kr = sems
    nz = at.nz
    core, z = at.core, at.z
    lanes = 128

    def chunk(i):
        return lax.rem(i + 2 * nz, nz)

    pz = zsend.shape[0]
    prow = tbuf.shape[3]

    def rows_of(t):
        return pl.ds(pl.multiple_of(t * prow, prow), prow)

    tiles = [
        remote(psum.at[:, :, rows_of(at.tile_at(d)), :], tbuf.at[at.t], ts.at[d], tr.at[d], at.s, at.tile_at(d))
        for d in range(1, nt)
    ]
    zcopies = [
        remote(zsend.at[lax.rem(z + d, pz)], zbuf.at[z], zs.at[d], zr.at[d], at.s_at_z(z + d), at.t)
        for d in range(1, nz)
    ]
    py = remote(pmine, pybuf, ms.at[3], mr.at[3], at.s_y, at.t)

    def core_stage():
        swap_p.wait_recv()
        psum[...] = pgrad[pl.ds(2 * core, 2)] + got_p[...]
        for copy in tiles:
            copy.start()
        tbuf[at.t] = psum[:, :, rows_of(at.t), :]

    def tile_stage():
        for copy in tiles:
            copy.wait_recv()
        total = tbuf[0]
        for t in range(1, nt):
            total = total + tbuf[t]
        zsend[...] = total.reshape(zsend.shape)
        for copy in zcopies:
            copy.start()
        zbuf[z] = zsend[lax.rem(z, pz)]

    def z_stage():
        for copy in zcopies:
            copy.wait_recv()
        total = zbuf[0]
        for j in range(1, nz):
            total = total + zbuf[j]
        pmine[...] = total
        py.start()

    def local(k, idx):
        return canvas[idx % 2, idx // 2, chunk(z + k)]

    chains = [(8, 1, 4, True), (-7, -1, 3, True), (4, 1, 4, False), (-4, -1, 4, False)]
    count = len(STREAMS)

    def target(q, i):
        return chains[q][0] - i * chains[q][1]

    def hop(q, i, p):
        _, way, hops, jumps = chains[q]
        part = pl.ds(*STREAMS[p])
        src = canvas.at[:, p, chunk(z + target(q, 0))] if i == 0 else chain.at[q, i - 1, part]
        to = target(q, i) if jumps and i == hops - 1 else way
        return remote(src, chain.at[q, i, part], us.at[q, i, p], ur.at[q, i, p], at.s_at_z(z + to), at.t)

    def span(p):
        return range(STREAMS[p][0], STREAMS[p][0] + STREAMS[p][1])

    for p in range(count):
        for q in range(4):
            hop(q, 0, p).start()
    core_stage()
    for i in range(4):
        for p in range(count):
            for q in range(4):
                if i < chains[q][2]:
                    hop(q, i, p).wait_recv()
                if i + 1 < chains[q][2]:
                    for idx in span(p):
                        chain[q, i, idx] += local(target(q, i + 1), idx)
                    hop(q, i + 1, p).start()
        if i == 1:
            tile_stage()
        if i == 2:
            z_stage()
    for idx in range(4):
        total = local(0, idx)
        for q in range(4):
            total = total + chain[q, chains[q][2] - 1, idx]
        mine[idx] = total

    to_y = remote(mine.at[pl.ds(0, 2)], ybuf, ms.at[0], mr.at[0], at.s_y, at.t)
    rim_a = remote(mine.at[pl.ds(2, 2)], rimbuf.at[0], ms.at[1], mr.at[1], at.s, at.tile_at(1))
    rim_b = remote(mine.at[pl.ds(2, 2)], rimbuf.at[1], ms.at[2], mr.at[2], at.s_y, at.tile_at(1))
    for rim in (rim_b, rim_a):
        pl.when(at.t < nt - 1)(rim.start)
    to_y.start()

    @pl.when(at.t == 0)
    def _():
        rimbuf[...] = jnp.zeros_like(rimbuf)

    py.wait_recv()
    gbuf[core, OWN, 8] = pmine[...] + pybuf[...]
    to_y.wait_recv()
    for rim in (rim_a, rim_b):
        pl.when(at.t > 0)(rim.wait_recv)
    for k in range(2):
        final = (mine[k] + ybuf[k]) + (rimbuf[0, k] + rimbuf[1, k])
        for l in range(4):
            gbuf[core, OWN, 4 * k + l] = final[:, lanes * l:lanes * (l + 1)]

    def pass_on(i, k, to, part=slice(0, 9)):
        new = k - to + 16 * (k - to < -OWN)
        part = pl.ds(part.start, part.stop - part.start)
        return remote(gbuf.at[core, k + OWN, part], gbuf.at[core, new + OWN, part], gs.at[i], gr.at[i], at.s_at_z(z + to), at.t)

    def share(k, lo, hi):
        part = gbuf.at[core, pl.ds(lo + OWN, hi - lo + 1)]
        return remote(part, part, ks.at[k], kr.at[k], at.s_core, at.t)

    top, low = slice(0, 4), slice(4, 9)
    far = [pass_on(0, 0, 6), pass_on(1, 0, -6)]
    near = [pass_on(2, 0, 1), pass_on(3, 0, -1), pass_on(4, 0, 2), pass_on(5, 0, -2)]
    after_near = [pass_on(6, 2, -1), pass_on(7, 2, -2), pass_on(8, -2, 1), pass_on(9, -2, 2)]
    after_far = [
        pass_on(10, 6, -1), pass_on(11, 6, 1), pass_on(12, 6, -2, top),
        pass_on(13, -6, 1), pass_on(14, -6, -1), pass_on(15, -6, 2, low),
    ]
    shares = [share(0, -2, 2), share(1, 3, 4), share(2, -4, -3), share(3, 5, 8), share(4, -7, -5)]
    for copy in far + near:
        copy.start()
    drain()
    for rim in (rim_a, rim_b):
        pl.when(at.t < nt - 1)(rim.wait_send)
    for copy in [to_y, py] + tiles + zcopies:
        copy.wait_send()
    for q in range(4):
        for i in range(chains[q][2]):
            for p in range(count):
                hop(q, i, p).wait_send()
    near[3].wait_recv()
    near[2].wait_recv()
    near[1].wait_recv()
    near[0].wait_recv()
    for copy in after_near:
        copy.start()
    far[0].wait_recv()
    far[1].wait_recv()
    for copy in after_far:
        copy.start()
    shares[0].start()
    for copy in after_near:
        copy.wait_recv()
    shares[1].start()
    shares[2].start()
    for copy in after_far:
        copy.wait_recv()
    shares[3].start()
    shares[4].start()
    for copy in shares:
        copy.wait_recv()

    for copy in far + near + after_near + after_far + shares:
        copy.wait_send()


def fused_kernel(ns, nt, off, spec, probe, meas_hbm, right_hbm, left_hbm, kern_hbm, gbuf, *scratch):
    ext, full, meas, right, left, kern, canvas, pgrad, xa, xb, ya, yb, patch, wave = scratch[:14]
    selecting, put_own, bufs, sems = scratch[14:22], scratch[22], scratch[23:34], scratch[34:]
    loads = [
        pltpu.make_async_copy(src, dst, sems[0].at[k])
        for k, (src, dst) in enumerate([(meas_hbm, meas), (right_hbm, right), (left_hbm, left), (kern_hbm, kern)])
    ]
    for copy in loads:
        copy.start()
    at = Place(ns, nt)
    z = at.z
    greet(
        [(s, at.tile_at(d)) for s in (at.s, at.s_y) for d in range(1, nt)]
        + [(at.s_at_z(z + d), at.t) for d in range(1, at.nz)] + [(at.s_y, at.t), (at.s_core, at.t)]
    )

    slots = slots_of(off, at.t, spec.shape[1])
    corners = sum(slots[1], ())
    lines = lax.broadcasted_iota(jnp.int32, put_own.shape, 0)
    places = jnp.zeros(put_own.shape, jnp.int32)
    for k, value in enumerate(corners):
        places = jnp.where(lines == k, value, places)
    put_own[...] = places
    wgrad, got_w, put_got = selecting[3], selecting[4], selecting[7]
    cs, cr = sems[10:12]
    swap_put = remote(put_own, put_got, cs.at[0], cr.at[0], at.s_core, at.t)
    swap_w = remote(wgrad.at[:, pl.ds(2 - 2 * at.core, 2)], got_w, cs.at[1], cr.at[1], at.s_core, at.t)
    swap_p = remote(pgrad.at[pl.ds(2 - 2 * at.core, 2)], bufs[0], cs.at[2], cr.at[2], at.s_core, at.t)

    def split_own():
        swap_put.start()
        split_rows(spec, selecting[0], 0, spec.shape[1], range(spec.shape[0]))

    share_later, finish, drain = gather_stage(at, nt, spec, probe, ext, full, sems[1:10], split_own)
    for copy in loads:
        copy.wait()
    window_stage(at, slots, off.shape[1], ext, full, meas, right, left, kern, canvas, pgrad, xa, xb, ya, yb, patch, wave, *selecting,
                 share_later, finish, swap_w, swap_p, swap_put)

    def drain_all():
        drain()
        for copy in (swap_put, swap_w, swap_p):
            copy.wait_send()

    sum_stage(at, nt, canvas, pgrad, gbuf, bufs, sems[12:], swap_p, drain_all)


def place_kernel(ns, nt, gbuf, out, pout):
    z = Place(ns, nt).z
    nz = gbuf.shape[1]
    lanes = gbuf.shape[4]
    for j in range(nz):
        slot = lax.rem(j - z + OWN + nz, nz)
        for c in range(2):
            for k in range(2):
                for l in range(4):
                    out[2 * c + k, j, :, lanes * l:lanes * (l + 1)] = gbuf[c, slot, 4 * k + l]
            if j < nz // 2:
                m, ri, h = j // 4, (j // 2) % 2, j % 2
                pout[2 * c + m, ri, pl.ds(8 * h, 8), :] = gbuf[c, slot, 8]


def shards(ns, nt, specimen, probe_modes, offsets, intensity):
    slices, two, height, width = specimen.shape
    modes, _, prow, n = probe_modes.shape
    planes = slices * two
    nz = ns // 4
    sub = height // nz
    count = len(STREAMS)
    right, left, kernel = dft_tables(n)
    dma = pltpu.SemaphoreType.DMA
    vmem = pl.BlockSpec(memory_space=pltpu.VMEM)
    hbm = pl.BlockSpec(memory_space=pl.ANY)

    def f32(*shape):
        return pltpu.VMEM(shape, F32)

    def pair(*shape):
        return [dma(shape), dma(shape)]

    gathered = pl.pallas_call(
        partial(fused_kernel, ns, nt),
        name="gradient_sums",
        out_shape=jax.ShapeDtypeStruct((2, nz, 9, 8, n), F32),
        in_specs=[pl.BlockSpec(memory_space=pltpu.SMEM), vmem, vmem] + [hbm] * 4,
        out_specs=vmem,
        scratch_shapes=[
            f32(planes, 2 * height, width),
            f32(modes * two, n, n),
            f32(*intensity.shape),
            pltpu.VMEM(right.shape, BF16),
            pltpu.VMEM(left.shape, BF16),
            f32(2, n, n),
            f32(2, 2, nz, sub, width),
            f32(modes, two, n, n),
            pltpu.VMEM((CAP * modes * n, 6 * n), BF16),
            pltpu.VMEM((CAP * modes * n, 6 * n), BF16),
            pltpu.VMEM((6 * n, CAP * modes * n), BF16),
            pltpu.VMEM((6 * n, CAP * modes * n), BF16),
            f32(CAP, planes, n, n),
            f32(CAP * modes, 2, n, n),
            pltpu.VMEM((2 * planes, 2 * height, width), BF16),
            pltpu.VMEM((width, CAP * n), BF16),
            pltpu.VMEM((CAP, 4 * height, planes * n), BF16),
            f32(CAP, planes, n, n),
            f32(CAP, 2, n, n),
            pltpu.VMEM((4 * height, 4 * CAP * n), BF16),
            pltpu.VMEM((4 * CAP * n, width), BF16),
            pltpu.VMEM((8, width), jnp.int32),
            pltpu.VMEM((8, width), jnp.int32),
            f32(2, two, n, n),
            f32(2, two, n, n),
            f32(nt, 2, two, prow, n),
            f32(2 * two * prow // 8, 8, n),
            f32(nz, 8, n),
            f32(8, n),
            f32(8, n),
            f32(4, 4, 4, sub, width),
            f32(4, sub, width),
            f32(2, sub, width),
            f32(2, 2, sub, width),
        ]
        + [dma((4,))]
        + [dma((3,))] + pair(2) + pair(nt) + pair(2, 4) + pair(3)
        + pair(3) + pair(4, 4, count) + pair(4) + pair(nt) + pair(nz) + pair(16) + pair(5),
        compiler_params=pltpu.CompilerParams(collective_id=0, has_side_effects=True, vmem_limit_bytes=VMEM_LIMIT),
    )(
        offsets, specimen.reshape(planes, height, width), probe_modes.reshape(modes * two, prow, n), intensity,
        jnp.asarray(right), jnp.asarray(left), jnp.asarray(kernel),
    )
    out, pout = pl.pallas_call(
        partial(place_kernel, ns, nt),
        name="place_rows",
        out_shape=(
            jax.ShapeDtypeStruct((planes, nz, sub, width), F32),
            jax.ShapeDtypeStruct((modes, two, prow, n), F32),
        ),
        in_specs=[vmem],
        out_specs=[vmem] * 2,
        compiler_params=pltpu.CompilerParams(vmem_limit_bytes=VMEM_LIMIT),
    )(gathered)
    return out.reshape(specimen.shape), pout


def solution(mesh):
    ns, nt = mesh.shape["scan"], mesh.shape["tile"]
    return jax.shard_map(
        partial(shards, ns, nt),
        mesh=mesh,
        in_specs=(
            P(None, None, "tile", None),
            P(None, None, "tile", None),
            P(None, "scan"),
            P("scan", None, None),
        ),
        out_specs=(P(None, None, "tile", None), P(None, None, "tile", None)),
        check_vma=False,
    )
```
